256 devices in a mesh: lat: 16 (over y, x_lo, core), lon: 16 (over z, x_hi).
Axes of the slice: x: 4 (x_hi: 2, x_lo: 2; x = x_hi * 2 + x_lo), y: 4, z: 8, core: 2. Of those that a mesh axis runs over, the one named last changes fastest.
Arguments:
- fields: bfloat16 [256, 128, 2048], P(None, 'lat', 'lon'), may hold values from -6 to 6
- grad_out: bfloat16 [256, 128, 2048], P(None, 'lat', 'lon'), may hold values from -6 to 6
- weight: bfloat16 [9, 256, 256], replicated, may hold values from -0.375 to 0.375
- basis_table: bfloat16 [9, 128, 7, 33], replicated, may hold values from -0.75 to 0.75
- lon_reach: int32 [128], replicated, may hold values from 1 to 16, as said below
Outputs:
- field_grad: bfloat16 [256, 128, 2048], P(None, 'lat', 'lon')
- weight_grad: float32 [9, 256, 256], replicated
The draws below stay inside these ranges and needn't reach their ends.
Inputs may be any that keep to these rules, and one draw needn't show every extreme that they name: lon_reach equals 16 on the rows nearest the poles, equals 1 on the rows farthest from both ends, and is larger near the poles than near the middle.
All inputs are finite; a program needn't handle non-finite values.
Results may differ from the reference program's by a relative error of at most 0.0049.
Values may be sent and summed in bfloat16 or wider, within the bound.
No kernel may reach another device: no remote copies, remote signals or barrier semaphores. Data moves between devices by JAX's collectives and lax.ppermute only.
A program may use at most 192 MiB of HBM per device.

```python
import jax
import jax.numpy as jnp
from jax import lax

C = 256
K = 9
R = 3
WMAX = 16
NLAT = 128
NLON = 2048


def draw_lon_reach(key, part):
    key = jax.random.fold_in(key, 11)
    row_ids = jnp.arange(NLAT, dtype=jnp.int32)
    distance = jnp.minimum(row_ids, NLAT - 1 - row_ids)
    jitter = jax.random.randint(key, (NLAT,), 0, 2, dtype=jnp.int32)
    reach = jnp.minimum(WMAX, 1 + 4 * WMAX // (distance + 4) + jitter)
    middle = (NLAT - 1) // 2
    reach = jnp.where(distance == middle, jnp.ones_like(reach), reach)
    return reach.astype(jnp.int32)


def levels(stream_key, extent, shards, least, high):
    factor_of, own = 1.0, jax.random.fold_in(stream_key, 6)
    for axis_at, blocks in shards:
        draws = jnp.exp(jax.random.uniform(jax.random.fold_in(own, axis_at), (blocks,), jnp.float32, least / len(shards), high / len(shards)))
        factor_of = factor_of * jnp.repeat(draws, extent[axis_at] // blocks).reshape([-1 if axis == axis_at else 1 for axis in range(len(extent))])
    return factor_of


def scatter_about(rng, dims, deviation, bound, shards=(), kind=jnp.bfloat16):
    values = jax.random.normal(rng, dims, jnp.float32) * deviation
    if len(shards) > 0:
        values = levels(rng, dims, shards, -0.22, 0.18) * values
    return jnp.clip(values, min=-bound, max=bound).astype(kind)


def setup_inputs(seed: int = 0) -> dict:
    key_list = jax.random.split(jax.random.key(seed), 6)
    fields = scatter_about(key_list[0], (C, NLAT, NLON), 1.0, 6.0, ((1, 16), (2, 16)))
    grad_out = scatter_about(key_list[1], (C, NLAT, NLON), 1.0, 6.0, ((1, 16), (2, 16)))
    weight = scatter_about(key_list[2], (K, C, C), C ** -0.5, 0.375)
    basis_table = scatter_about(key_list[3], (K, NLAT, 2 * R + 1, 2 * WMAX + 1), (8 * (2 * R + 1)) ** -0.5, 0.75)
    lon_reach = draw_lon_reach(jax.random.fold_in(key_list[5], 71), 0)
    return {"fields": fields, "grad_out": grad_out, "weight": weight, "basis_table": basis_table, "lon_reach": lon_reach}


def masked_basis(basis_table, lon_reach):
    tap_count = basis_table.shape[3]
    col_half = (tap_count - 1) // 2
    offset = jnp.abs(lax.iota(jnp.int32, tap_count) - col_half)
    keeping = offset[None, :] <= lon_reach[:, None]
    return jnp.where(keeping[None, :, None, :], basis_table, jnp.zeros_like(basis_table))


def reference(fields, grad_out, weight, basis_table, lon_reach):
    highest = lax.Precision.HIGHEST
    masked = masked_basis(basis_table, lon_reach).astype(jnp.float32)
    channels, nlat_all, nlon_all = fields.shape
    basis_count, unused, row_span, tap_count = basis_table.shape
    row_half = (row_span - 1) // 2
    col_half = (tap_count - 1) // 2
    numbers = ("NCH", "OIH", "NCH")
    row_ids = jnp.arange(nlat_all, dtype=jnp.int32)

    fields_pad = jnp.pad(fields.astype(jnp.float32), ((0, 0), (row_half, row_half), (0, 0)))
    fields_pad = jnp.concatenate([fields_pad[:, :, nlon_all - col_half:], fields_pad, fields_pad[:, :, :col_half]], axis=2)
    grad_f = grad_out.astype(jnp.float32)
    weight_f = weight.astype(jnp.float32)

    def grad_row(running, row):
        window = lax.dynamic_slice_in_dim(fields_pad, row, row_span, 1)
        kernel = lax.dynamic_index_in_dim(masked, row, 1, keepdims=False)
        response = lax.conv_general_dilated(window, kernel, (1,), "VALID", dimension_numbers=numbers, precision=highest)
        response = lax.optimization_barrier(response.astype(jnp.bfloat16)).astype(jnp.float32)
        target = lax.dynamic_index_in_dim(grad_f, row, 1, keepdims=False)
        return running + jnp.einsum("ckl,dl->kcd", response, target, precision=highest), None

    start = jnp.zeros((basis_count, channels, channels), jnp.float32)
    weight_grad = lax.scan(grad_row, start, row_ids)[0] / nlat_all

    def mix_row(row):
        target = lax.dynamic_index_in_dim(grad_f, row, 1, keepdims=False)
        return jnp.einsum("kcd,dl->kcl", weight_f, target, precision=highest).astype(jnp.bfloat16)

    mixed = lax.map(mix_row, row_ids)
    mixed_pad = jnp.pad(mixed, ((row_half, row_half), (0, 0), (0, 0), (0, 0)))
    mixed_pad = jnp.concatenate([mixed_pad[:, :, :, nlon_all - col_half:], mixed_pad, mixed_pad[:, :, :, :col_half]], axis=3)
    basis_pad = jnp.pad(masked, ((0, 0), (row_half, row_half), (0, 0), (0, 0)))

    def back_row(row):
        z_window = lax.dynamic_slice_in_dim(mixed_pad, row, row_span, 0).astype(jnp.float32)[::-1]
        stacked_in = jnp.transpose(z_window, (2, 1, 0, 3)).reshape(channels, basis_count * row_span, -1)
        basis_rows = lax.dynamic_slice_in_dim(basis_pad, row, row_span, 1)
        flipped = jnp.stack([basis_rows[:, 2 * row_half - shift_row, shift_row, :] for shift_row in range(row_span)], axis=1)
        flipped = jnp.flip(flipped, 2).reshape(1, basis_count * row_span, tap_count)
        result = lax.conv_general_dilated(stacked_in, flipped, (1,), "VALID", dimension_numbers=numbers, precision=highest)
        return result[:, 0, :].astype(jnp.bfloat16)

    field_grad = jnp.transpose(lax.map(back_row, row_ids), (1, 0, 2))
    return field_grad, weight_grad
```

```python
import jax
import jax.numpy as jnp
from jax import lax
from jax.experimental import pallas as pl
from jax.experimental.pallas import tpu as pltpu
from jax.sharding import Mesh, PartitionSpec as P

LAT = ("y", "x_lo", "core")
LON = ("z", "x_hi")
PLANE = ("y", "x_hi", "x_lo")
BLOCK = 32
bf16, f32 = jnp.bfloat16, jnp.float32


def shift(x, axes, step, closed):
    count = 1
    for axis in axes:
        count *= lax.axis_size(axis)
    pairs = [(i, (i + step) % count) for i in range(count) if closed or 0 <= i + step < count]
    return lax.ppermute(x, axes, pairs)


def tap_rows(basis_table, lon_reach, first_row, lat_dev):
    basis_count, nlat_all, row_span, tap_count = basis_table.shape
    half = row_span // 2
    near = lat_dev + 2 * half
    start = jnp.clip(first_row - half, 0, nlat_all - near)
    table = lax.dynamic_slice_in_dim(basis_table, start, near, 1)
    reach = lax.dynamic_slice_in_dim(lon_reach, start, near, 0)
    offset = jnp.abs(lax.iota(jnp.int32, tap_count) - tap_count // 2)
    table = jnp.where((offset[None, :] <= reach[:, None])[None, :, None, :], table, jnp.zeros_like(table))
    table = jnp.pad(table, ((0, 0), (half, half), (0, 0), (0, 0)))
    table = lax.dynamic_slice_in_dim(table, first_row - start, near, 1)
    table = jnp.flip(table, 3)
    rows = jnp.stack(
        [table[:, s : s + lat_dev, row_span - 1 - s, :] for s in range(row_span)], axis=2
    )
    rows = jnp.pad(rows, ((0, 0), (0, 0), (0, 1), (0, 2 * BLOCK - tap_count)))
    rows = jnp.transpose(rows, (1, 0, 2, 3)).astype(f32)
    return rows.reshape(lat_dev, basis_count, (row_span + 1) * BLOCK * 2 // 128, 128)


def spread_kernel(core_ref, main, up, down, left, right, taps, f_ref, q_ref, keep, send, ext, band):
    lat_dev, lon_dev, channels = main.shape
    half = up.shape[0]
    basis_count, groups = taps.shape[1], taps.shape[2]
    side = left.shape[1]
    row_span = 2 * half + 1
    ext[:half, side : side + lon_dev, :] = up[...]
    ext[half : half + lat_dev, side : side + lon_dev, :] = main[...]
    ext[half + lat_dev :, side : side + lon_dev, :] = down[...]
    ext[:, :side, :] = left[...]
    ext[:, side + lon_dev :, :] = right[...]

    def row(i, carry):
        for k in range(basis_count):
            for p in range(groups):
                line = jnp.broadcast_to(taps[i, k, p : p + 1, :], (BLOCK, 128))
                line = pltpu.roll(line, 0, 1, stride=1, stride_axis=0)
                band[k * BLOCK : (k + 1) * BLOCK, p * 128 : (p + 1) * 128] = line.astype(bf16)
        for j in range(lon_dev // BLOCK):
            parts = [ext[i + s, j * BLOCK : (j + 2) * BLOCK, :] for s in range(row_span)]
            window = jnp.concatenate(parts + [jnp.zeros_like(parts[0])], axis=0)
            out = jnp.dot(band[...], window, preferred_element_type=f32).astype(bf16)
            for k in range(basis_count):
                at = pl.ds(pl.multiple_of(i * lon_dev + j * BLOCK, BLOCK), BLOCK)
                q_ref[k, at, :] = out[k * BLOCK : (k + 1) * BLOCK, :]
        return carry

    lax.fori_loop(0, lat_dev, row, 0)
    first = core_ref[0] == 0

    def grad(k, carry):
        out = jnp.dot(f_ref[...], q_ref[k], preferred_element_type=f32)
        low, high = out[:, : channels // 2], out[:, channels // 2 :]
        keep[k] = jnp.where(first, low, high)
        send[k] = jnp.where(first, high, low)
        return carry

    lax.fori_loop(0, basis_count, grad, 0)


def spread(core, main, up, down, left, right, taps, cells):
    lat_dev, lon_dev, channels = main.shape
    basis_count = taps.shape[1]
    near, wide = lat_dev + 2 * up.shape[0], lon_dev + 2 * left.shape[1]
    vmem = pl.BlockSpec(memory_space=pltpu.VMEM)
    half = jax.ShapeDtypeStruct((basis_count, channels, channels // 2), f32)
    return pl.pallas_call(
        spread_kernel,
        out_shape=(jax.ShapeDtypeStruct((basis_count, lat_dev * lon_dev, channels), bf16), half, half),
        in_specs=[pl.BlockSpec(memory_space=pltpu.SMEM)] + [vmem] * 7,
        out_specs=(vmem, vmem, vmem),
        scratch_shapes=[
            pltpu.VMEM((near, wide, channels), bf16),
            pltpu.VMEM((basis_count * BLOCK, taps.shape[2] * 128), bf16),
        ],
        compiler_params=pltpu.CompilerParams(vmem_limit_bytes=40 * 1024 * 1024),
        cost_estimate=pl.CostEstimate(flops=4 * 10**9, bytes_accessed=10**7, transcendentals=0),
    )(core, main, up, down, left, right, taps, cells)


def mix_kernel(w_ref, q_ref, out_ref):
    basis_count, cells, channels = q_ref.shape

    def part(j, carry):
        at = pl.ds(pl.multiple_of(j * 256, 256), 256)
        total = jnp.zeros((channels, 256), f32)
        for k in range(basis_count):
            total += lax.dot_general(
                w_ref[k], q_ref[k, at, :], (((1,), (1,)), ((), ())), preferred_element_type=f32
            )
        out_ref[:, at] = total.astype(bf16)
        return carry

    lax.fori_loop(0, cells // 256, part, 0)


def mix(weight, q):
    basis_count, cells, channels = q.shape
    vmem = pl.BlockSpec(memory_space=pltpu.VMEM)
    return pl.pallas_call(
        mix_kernel,
        out_shape=jax.ShapeDtypeStruct((channels, cells), bf16),
        in_specs=[vmem, vmem],
        out_specs=vmem,
        compiler_params=pltpu.CompilerParams(vmem_limit_bytes=30 * 1024 * 1024),
        cost_estimate=pl.CostEstimate(flops=12 * 10**8, bytes_accessed=7 * 10**6, transcendentals=0),
    )(weight, q)


def all_to_all(x, axes):
    return lax.all_to_all(x, axes, 0, 0, tiled=True)


def to_all(x, count):
    return jnp.broadcast_to(x[None], (count,) + x.shape)


def reduce_all(keep, send, core, scale):
    swap = [(0, 1), (1, 0)]
    basis_count, channels, half = keep.shape
    plane = 1
    for axis in PLANE:
        plane *= lax.axis_size(axis)
    depth = lax.axis_size("z")
    own = keep + lax.ppermute(send, "core", swap)
    own = own.reshape(plane, -1, half).astype(bf16)
    own = jnp.sum(all_to_all(own, PLANE).astype(f32), axis=0).astype(bf16)
    own = jnp.sum(all_to_all(to_all(own, depth), ("z",)).astype(f32), axis=0)
    own = (own * scale).astype(bf16)
    own = all_to_all(to_all(own, plane), PLANE).reshape(basis_count, channels, half)
    other = lax.ppermute(own, "core", swap)
    low, high = jnp.where(core == 0, own, other), jnp.where(core == 0, other, own)
    return jnp.concatenate([low, high], axis=2).astype(f32)


def local(fields, grad_out, weight, basis_table, lon_reach):
    channels, lat_dev, lon_dev = fields.shape
    nlat_all = basis_table.shape[1]
    half, side = basis_table.shape[2] // 2, basis_table.shape[3] // 2
    core = lax.axis_index("core")
    taps = tap_rows(basis_table, lon_reach, lax.axis_index(LAT) * lat_dev, lat_dev)
    main = jnp.transpose(grad_out, (1, 2, 0))
    up = shift(main[lat_dev - half :], LAT, 1, False)
    down = shift(main[:half], LAT, -1, False)
    tall = lambda at: jnp.concatenate([up[:, at], main[:, at], down[:, at]], axis=0)
    left = shift(tall(slice(lon_dev - side, lon_dev)), LON, 1, True)
    right = shift(tall(slice(0, side)), LON, -1, True)
    cells = fields.reshape(channels, lat_dev * lon_dev)
    q, keep, send = spread(core[None].astype(jnp.int32), main, up, down, left, right, taps, cells)
    field_grad = mix(weight, q).reshape(channels, lat_dev, lon_dev)
    weight_grad = reduce_all(keep, send, core, 1.0 / nlat_all)
    return field_grad, weight_grad


def solution(mesh):
    fine = Mesh(mesh.devices.reshape(4, 2, 2, 8, 2), ("y", "x_lo", "core", "z", "x_hi"))
    split = P(None, LAT, LON)
    return jax.shard_map(
        local,
        mesh=fine,
        in_specs=(split, split, P(), P(), P()),
        out_specs=(split, P()),
        check_vma=False,
    )
```

```python
import jax
import jax.numpy as jnp
from jax import lax
from jax.experimental import pallas as pl
from jax.experimental.pallas import tpu as pltpu
from jax.sharding import Mesh, PartitionSpec as P

LAT = ("y", "x_lo", "core")
LON = ("z", "x_hi")
PLANE = ("y", "x_hi", "x_lo")
BLOCK = 32
bf16, f32 = jnp.bfloat16, jnp.float32


def shift(x, axes, step, closed):
    count = 1
    for axis in axes:
        count *= lax.axis_size(axis)
    pairs = [(i, (i + step) % count) for i in range(count) if closed or 0 <= i + step < count]
    return lax.ppermute(x, axes, pairs)


def tap_rows(basis_table, lon_reach, first_row, lat_dev):
    basis_count, nlat_all, row_span, tap_count = basis_table.shape
    half = row_span // 2
    near = lat_dev + 2 * half
    start = jnp.clip(first_row - half, 0, nlat_all - near)
    table = lax.dynamic_slice_in_dim(basis_table, start, near, 1)
    reach = lax.dynamic_slice_in_dim(lon_reach, start, near, 0)
    offset = jnp.abs(lax.iota(jnp.int32, tap_count) - tap_count // 2)
    table = jnp.where((offset[None, :] <= reach[:, None])[None, :, None, :], table, jnp.zeros_like(table))
    table = jnp.pad(table, ((0, 0), (half, half), (0, 0), (0, 0)))
    table = lax.dynamic_slice_in_dim(table, first_row - start, near, 1)
    table = jnp.flip(table, 3)
    rows = jnp.stack(
        [table[:, s : s + lat_dev, row_span - 1 - s, :] for s in range(row_span)], axis=2
    )
    rows = jnp.pad(rows, ((0, 0), (0, 0), (0, 1), (0, 2 * BLOCK - tap_count)))
    rows = jnp.transpose(rows, (1, 0, 2, 3)).astype(f32)
    return rows.reshape(lat_dev, basis_count, (row_span + 1) * BLOCK * 2 // 128, 128)


def band_kernel(taps, band):
    lat_dev, basis_count, groups, _ = taps.shape
    for i in range(lat_dev):
        for k in range(basis_count):
            for p in range(groups):
                line = jnp.broadcast_to(taps[i, k, p : p + 1, :], (BLOCK, 128))
                line = pltpu.roll(line, 0, 1, stride=1, stride_axis=0)
                band[i, k * BLOCK : (k + 1) * BLOCK, p * 128 : (p + 1) * 128] = line.astype(bf16)


def convolve(band, ext, place, q_ref):
    basis_count, lat_dev, columns, _ = q_ref.shape
    row_span = ext.shape[0] - lat_dev + 1
    for i in range(lat_dev):
        for j in range(columns // BLOCK):
            parts = [ext[(i + s,) + place(j)] for s in range(row_span)]
            window = jnp.concatenate(parts + [jnp.zeros_like(parts[0])], axis=0)
            out = jnp.dot(band[i], window, preferred_element_type=f32).astype(bf16)
            for k in range(basis_count):
                q_ref[k, i, j * BLOCK : (j + 1) * BLOCK, :] = out[k * BLOCK : (k + 1) * BLOCK, :]


def middle_kernel(band, main, up, down, f_ref, q_ref, total, ext):
    lat_dev, half = main.shape[0], up.shape[0]
    ext[:half] = up[...]
    ext[half : half + lat_dev] = main[...]
    ext[half + lat_dev :] = down[...]
    side = BLOCK // 2
    convolve(band, ext, lambda j: (slice(side + j * BLOCK, side + (j + 2) * BLOCK),), q_ref)
    for k in range(q_ref.shape[0]):
        cells = q_ref[k].reshape(f_ref.shape[1], q_ref.shape[3])
        total[k] = jnp.dot(f_ref[...], cells, preferred_element_type=f32)


def edge_kernel(core_ref, band, main, up, down, left, right, f_ref, total, q_ref, keep, send, ext):
    lat_dev, lon_dev, channels = main.shape
    half, side = up.shape[0], left.shape[1]
    inner = 2 * BLOCK - side
    for first, last, source in ((0, half, up), (half, half + lat_dev, main), (half + lat_dev, 2 * half + lat_dev, down)):
        ext[first:last, 0, side:, :] = source[:, :inner, :]
        ext[first:last, 1, :inner, :] = source[:, lon_dev - inner :, :]
    ext[:, 0, :side, :] = left[...]
    ext[:, 1, inner:, :] = right[...]
    convolve(band, ext, lambda j: (j,), q_ref)
    low_core = core_ref[0] == 0
    for k in range(q_ref.shape[0]):
        cells = q_ref[k].reshape(f_ref.shape[1], channels)
        out = total[k] + jnp.dot(f_ref[...], cells, preferred_element_type=f32)
        low, high = out[:, : channels // 2], out[:, channels // 2 :]
        keep[k] = jnp.where(low_core, low, high)
        send[k] = jnp.where(low_core, high, low)


def call(kernel, out_shape, operands, scratch=(), scalars=0, flops=10**9):
    vmem = pl.BlockSpec(memory_space=pltpu.VMEM)
    smem = pl.BlockSpec(memory_space=pltpu.SMEM)
    return pl.pallas_call(
        kernel,
        out_shape=out_shape,
        in_specs=[smem] * scalars + [vmem] * (len(operands) - scalars),
        out_specs=jax.tree.map(lambda _: vmem, out_shape),
        scratch_shapes=list(scratch),
        compiler_params=pltpu.CompilerParams(vmem_limit_bytes=40 * 1024 * 1024),
        cost_estimate=pl.CostEstimate(flops=flops, bytes_accessed=10**6, transcendentals=0),
    )(*operands)


def mix_kernel(w_ref, mid_ref, edge_ref, out_ref):
    basis_count, lat_dev, columns, channels = mid_ref.shape
    for i in range(0, lat_dev, 2):
        total = jnp.zeros((channels, 4 * columns), f32)
        for k in range(basis_count):
            parts = []
            for row in (i, i + 1):
                parts += [edge_ref[k, row, :BLOCK], mid_ref[k, row], edge_ref[k, row, BLOCK:]]
            total += lax.dot_general(
                w_ref[k], jnp.concatenate(parts, axis=0), (((1,), (1,)), ((), ())), preferred_element_type=f32
            )
        out_ref[:, i * 2 * columns : (i + 2) * 2 * columns] = total.astype(bf16)


def all_to_all(x, axes):
    return lax.all_to_all(x, axes, 0, 0, tiled=True)


def to_all(x, count):
    return jnp.broadcast_to(x[None], (count,) + x.shape)


def reduce_all(keep, send, core, scale, beside):
    swap = [(0, 1), (1, 0)]
    basis_count, channels, half = keep.shape
    plane = 1
    for axis in PLANE:
        plane *= lax.axis_size(axis)
    depth = lax.axis_size("z")
    came, beside = lax.optimization_barrier((lax.ppermute(send, "core", swap), beside))
    own = keep + came
    own = own.reshape(plane, -1, half).astype(bf16)
    own = jnp.sum(all_to_all(own, PLANE).astype(f32), axis=0).astype(bf16)
    own = jnp.sum(all_to_all(to_all(own, depth), ("z",)).astype(f32), axis=0)
    own = (own * scale).astype(bf16)
    own = all_to_all(to_all(own, plane), PLANE).reshape(basis_count, channels, half)
    other = lax.ppermute(own, "core", swap)
    low, high = jnp.where(core == 0, own, other), jnp.where(core == 0, other, own)
    return jnp.concatenate([low, high], axis=2).astype(f32), beside


def local(fields, grad_out, weight, basis_table, lon_reach):
    channels, lat_dev, lon_dev = fields.shape
    nlat_all = basis_table.shape[1]
    half, side = basis_table.shape[2] // 2, basis_table.shape[3] // 2
    core = lax.axis_index("core")
    taps = tap_rows(basis_table, lon_reach, lax.axis_index(LAT) * lat_dev, lat_dev)
    main = jnp.transpose(grad_out, (1, 2, 0))
    up = shift(main[lat_dev - half :], LAT, 1, False)
    down = shift(main[:half], LAT, -1, False)
    tall = lambda at: jnp.concatenate([up[:, at], main[:, at], down[:, at]], axis=0)
    left = shift(tall(slice(lon_dev - side, lon_dev)), LON, 1, True)
    right = shift(tall(slice(0, side)), LON, -1, True)
    basis_count = basis_table.shape[0]
    near = lat_dev + 2 * half
    wide = 2 * BLOCK
    f_mid = fields[:, :, BLOCK : lon_dev - BLOCK].reshape(channels, lat_dev * wide)
    f_edge = jnp.concatenate([fields[:, :, :BLOCK], fields[:, :, lon_dev - BLOCK :]], axis=2)
    f_edge = f_edge.reshape(channels, lat_dev * wide)
    shape = jax.ShapeDtypeStruct
    q_shape = shape((basis_count, lat_dev, wide, channels), bf16)
    part = shape((basis_count, channels, channels // 2), f32)
    band_shape = shape((lat_dev, basis_count * BLOCK, taps.shape[2] * 128), bf16)
    band = call(band_kernel, band_shape, (taps,))
    q_mid, total = call(
        middle_kernel,
        (q_shape, shape((basis_count, channels, channels), f32)),
        (band, main, up, down, f_mid),
        [pltpu.VMEM((near, lon_dev, channels), bf16)],
    )
    q_edge, keep, send = call(
        edge_kernel,
        (q_shape, part, part),
        (core[None].astype(jnp.int32), band, main, up, down, left, right, f_edge, total),
        [pltpu.VMEM((near, 2, wide, channels), bf16)],
        scalars=1,
    )
    mixed = call(mix_kernel, shape((channels, lat_dev * lon_dev), bf16), (weight, q_mid, q_edge))
    field_grad = mixed.reshape(channels, lat_dev, lon_dev)
    weight_grad, field_grad = reduce_all(keep, send, core, 1.0 / nlat_all, field_grad)
    return field_grad, weight_grad


def solution(mesh):
    fine = Mesh(mesh.devices.reshape(4, 2, 2, 8, 2), ("y", "x_lo", "core", "z", "x_hi"))
    split = P(None, LAT, LON)
    return jax.shard_map(
        local,
        mesh=fine,
        in_specs=(split, split, P(), P(), P()),
        out_specs=(split, P()),
        check_vma=False,
    )
```

```python
import jax
import jax.numpy as jnp
from jax import lax
from jax.experimental import pallas as pl
from jax.experimental.pallas import tpu as pltpu
from jax.sharding import Mesh, PartitionSpec as P

LAT = ("y", "x_lo", "core")
LON = ("z", "x_hi")
PLANE = ("y", "x_hi", "x_lo")
BLOCK = 32
bf16, f32 = jnp.bfloat16, jnp.float32


def shift(x, axes, step, closed):
    count = 1
    for axis in axes:
        count *= lax.axis_size(axis)
    pairs = [(i, (i + step) % count) for i in range(count) if closed or 0 <= i + step < count]
    return lax.ppermute(x, axes, pairs)


def tap_rows(basis_table, lon_reach, start, near):
    basis_count, _, row_span, tap_count = basis_table.shape
    table = lax.dynamic_slice_in_dim(basis_table, start, near, 1)
    reach = lax.dynamic_slice_in_dim(lon_reach, start, near, 0)
    offset = jnp.abs(lax.iota(jnp.int32, tap_count) - tap_count // 2)
    table = jnp.where((offset[None, :] <= reach[:, None])[None, :, None, :], table, jnp.zeros_like(table))
    table = jnp.flip(table, (2, 3)).astype(f32)
    table = jnp.pad(table, ((0, 0), (0, 0), (0, 1), (0, 2 * BLOCK - tap_count)))
    table = jnp.transpose(table, (1, 0, 2, 3))
    return table.reshape(near, basis_count, (row_span + 1) * BLOCK * 2 // 128, 128)


def prepare_kernel(off_ref, taps, f_ref, band, f_mid, f_edge):
    near, basis_count, groups, _ = taps.shape
    lat_dev = band.shape[0]
    lane = lax.broadcasted_iota(jnp.int32, (1, 128), 1)
    rows = [jnp.clip(off_ref[0] + r, 0, near - 1) for r in range(near + 1)]
    for i in range(lat_dev):
        for k in range(basis_count):
            for p in range(groups):
                first = taps[rows[i + 2 * p], k, p : p + 1, :]
                second = taps[rows[i + 2 * p + 1], k, p : p + 1, :]
                line = jnp.broadcast_to(jnp.where(lane < 2 * BLOCK, first, second), (BLOCK, 128))
                line = pltpu.roll(line, 0, 1, stride=1, stride_axis=0)
                band[i, k * BLOCK : (k + 1) * BLOCK, p * 128 : (p + 1) * 128] = line.astype(bf16)
    for i in range(0, lat_dev, 2):
        even = f_ref[:, i * 128 : (i + 1) * 128].astype(f32)
        odd = f_ref[:, (i + 1) * 128 : (i + 2) * 128].astype(f32)
        back = lambda x: pltpu.roll(x, 128 - BLOCK, 1)
        ahead = lambda x: pltpu.roll(x, BLOCK, 1)
        at = slice(i * 64, (i + 2) * 64)
        f_mid[:, at] = jnp.where(lane < 64, back(even), ahead(odd)).astype(bf16)
        f_edge[:, at] = jnp.where(lane < 64, ahead(even), back(odd)).astype(bf16)


def rim_kernel(main, up, down, tail, head):
    half, lat_dev, side = up.shape[0], main.shape[0], tail.shape[1]
    last = main.shape[1] - side
    tail[:half] = up[:, last:, :]
    tail[half : half + lat_dev] = main[:, last:, :]
    tail[half + lat_dev :] = down[:, last:, :]
    head[:half] = up[:, :side, :]
    head[half : half + lat_dev] = main[:, :side, :]
    head[half + lat_dev :] = down[:, :side, :]


def convolve(band, ext, place, q_ref):
    basis_count, lat_dev, columns, _ = q_ref.shape
    row_span = ext.shape[0] - lat_dev + 1
    for i in range(lat_dev):
        for j in range(columns // BLOCK):
            parts = [ext[(i + s,) + place(j)] for s in range(row_span)]
            window = jnp.concatenate(parts + [jnp.zeros_like(parts[0])], axis=0)
            out = jnp.dot(band[i], window, preferred_element_type=f32).astype(bf16)
            for k in range(basis_count):
                q_ref[k, i, j * BLOCK : (j + 1) * BLOCK, :] = out[k * BLOCK : (k + 1) * BLOCK, :]


def middle_kernel(band, main, up, down, f_ref, q_ref, total, ext):
    lat_dev, half = main.shape[0], up.shape[0]
    ext[:half] = up[...]
    ext[half : half + lat_dev] = main[...]
    ext[half + lat_dev :] = down[...]
    side = BLOCK // 2
    convolve(band, ext, lambda j: (slice(side + j * BLOCK, side + (j + 2) * BLOCK),), q_ref)
    for k in range(q_ref.shape[0]):
        cells = q_ref[k].reshape(f_ref.shape[1], q_ref.shape[3])
        total[k] = jnp.dot(f_ref[...], cells, preferred_element_type=f32)


def edge_kernel(band, main, up, down, left, right, f_ref, total, q_ref, low, high, ext):
    lat_dev, lon_dev, channels = main.shape
    half, side = up.shape[0], left.shape[1]
    inner = 2 * BLOCK - side
    for first, last, source in ((0, half, up), (half, half + lat_dev, main), (half + lat_dev, 2 * half + lat_dev, down)):
        ext[first:last, 0, :inner, :] = source[:, lon_dev - inner :, :]
        ext[first:last, 1, side:, :] = source[:, :inner, :]
    ext[:, 0, inner:, :] = right[...]
    ext[:, 1, :side, :] = left[...]
    convolve(band, ext, lambda j: (j,), q_ref)
    for k in range(q_ref.shape[0]):
        cells = q_ref[k].reshape(f_ref.shape[1], channels)
        out = total[k] + jnp.dot(f_ref[...], cells, preferred_element_type=f32)
        low[k] = out[:, : channels // 2]
        high[k] = out[:, channels // 2 :]


def call(kernel, out_shape, operands, scratch=(), scalars=0, flops=10**9):
    vmem = pl.BlockSpec(memory_space=pltpu.VMEM)
    smem = pl.BlockSpec(memory_space=pltpu.SMEM)
    return pl.pallas_call(
        kernel,
        out_shape=out_shape,
        in_specs=[smem] * scalars + [vmem] * (len(operands) - scalars),
        out_specs=jax.tree.map(lambda _: vmem, out_shape),
        scratch_shapes=list(scratch),
        compiler_params=pltpu.CompilerParams(vmem_limit_bytes=40 * 1024 * 1024),
        cost_estimate=pl.CostEstimate(flops=flops, bytes_accessed=10**6, transcendentals=0),
    )(*operands)


def mix_kernel(w_ref, mid_ref, edge_ref, out_ref):
    basis_count, lat_dev, columns, channels = mid_ref.shape
    for i in range(0, lat_dev, 2):
        total = jnp.zeros((channels, 4 * columns), f32)
        for k in range(basis_count):
            parts = []
            for row in (i, i + 1):
                parts += [edge_ref[k, row, BLOCK:], mid_ref[k, row], edge_ref[k, row, :BLOCK]]
            total += lax.dot_general(
                w_ref[k], jnp.concatenate(parts, axis=0), (((1,), (1,)), ((), ())), preferred_element_type=f32
            )
        out_ref[:, i * 2 * columns : (i + 2) * 2 * columns] = total.astype(bf16)


def all_to_all(x, axes):
    return lax.all_to_all(x, axes, 0, 0, tiled=True)


def to_all(x, count):
    return jnp.broadcast_to(x[None], (count,) + x.shape)


def reduce_all(low, high, core, scale, beside):
    swap = [(0, 1), (1, 0)]
    basis_count, channels, half = low.shape
    plane = 1
    for axis in PLANE:
        plane *= lax.axis_size(axis)
    depth = lax.axis_size("z")
    keep, send = jnp.where(core == 0, low, high), jnp.where(core == 0, high, low)
    came, beside = lax.optimization_barrier((lax.ppermute(send, "core", swap), beside))
    own = keep + came
    own = own.reshape(plane, -1, half).astype(bf16)
    own = jnp.sum(all_to_all(own, PLANE).astype(f32), axis=0).astype(bf16)
    own = jnp.sum(all_to_all(to_all(own, depth), ("z",)).astype(f32), axis=0)
    own = (own * scale).astype(bf16)
    own = all_to_all(to_all(own, plane), PLANE).reshape(basis_count, channels, half)
    other = lax.ppermute(own, "core", swap)
    low, high = jnp.where(core == 0, own, other), jnp.where(core == 0, other, own)
    return jnp.concatenate([low, high], axis=2).astype(f32), beside


def local(fields, grad_out, weight, basis_table, lon_reach):
    channels, lat_dev, lon_dev = fields.shape
    basis_count, nlat_all, row_span, tap_count = basis_table.shape
    half, side = row_span // 2, tap_count // 2
    near, wide = lat_dev + 2 * half, 2 * BLOCK
    shape = jax.ShapeDtypeStruct
    core = lax.axis_index("core")
    main = jnp.transpose(grad_out, (1, 2, 0))
    up = shift(main[lat_dev - half :], LAT, 1, False)
    down = shift(main[:half], LAT, -1, False)
    rim = shape((near, side, channels), bf16)
    tail, head = call(rim_kernel, (rim, rim), (main, up, down), flops=10**6)
    left = shift(tail, LON, 1, True)
    right = shift(head, LON, -1, True)
    above = lax.axis_index(LAT) * lat_dev - half
    start = jnp.clip(above, 0, nlat_all - near)
    taps = tap_rows(basis_table, lon_reach, start, near)
    band, f_mid, f_edge = call(
        prepare_kernel,
        (
            shape((lat_dev, basis_count * BLOCK, taps.shape[2] * 128), bf16),
            shape((channels, lat_dev * wide), bf16),
            shape((channels, lat_dev * wide), bf16),
        ),
        ((above - start)[None], taps, fields.reshape(channels, lat_dev * lon_dev)),
        scalars=1,
    )
    q_shape = shape((basis_count, lat_dev, wide, channels), bf16)
    part = shape((basis_count, channels, channels // 2), f32)
    q_mid, total = call(
        middle_kernel,
        (q_shape, shape((basis_count, channels, channels), f32)),
        (band, main, up, down, f_mid),
        [pltpu.VMEM((near, lon_dev, channels), bf16)],
    )
    q_edge, low, high = call(
        edge_kernel,
        (q_shape, part, part),
        (band, main, up, down, left, right, f_edge, total),
        [pltpu.VMEM((near, 2, wide, channels), bf16)],
    )
    mixed = call(mix_kernel, shape((channels, lat_dev * lon_dev), bf16), (weight, q_mid, q_edge))
    field_grad = mixed.reshape(channels, lat_dev, lon_dev)
    weight_grad, field_grad = reduce_all(low, high, core, 1.0 / nlat_all, field_grad)
    return field_grad, weight_grad


def solution(mesh):
    fine = Mesh(mesh.devices.reshape(4, 2, 2, 8, 2), ("y", "x_lo", "core", "z", "x_hi"))
    split = P(None, LAT, LON)
    return jax.shard_map(
        local,
        mesh=fine,
        in_specs=(split, split, P(), P(), P()),
        out_specs=(split, P()),
        check_vma=False,
    )
```

```python
import jax
import jax.numpy as jnp
from jax import lax
from jax.experimental import pallas as pl
from jax.experimental.pallas import tpu as pltpu
from jax.sharding import Mesh, PartitionSpec as P

LAT = ("y", "x_lo", "core")
LON = ("z", "x_hi")
PLANE = ("y", "x_hi", "x_lo")
BLOCK = 32
bf16, f32 = jnp.bfloat16, jnp.float32


def shift(x, axes, step, closed):
    count = 1
    for axis in axes:
        count *= lax.axis_size(axis)
    pairs = [(i, (i + step) % count) for i in range(count) if closed or 0 <= i + step < count]
    return lax.ppermute(x, axes, pairs)


def tap_rows(basis_table, lon_reach, start, near):
    tap_count = basis_table.shape[3]
    table = lax.dynamic_slice_in_dim(basis_table, start, near, 1)
    reach = lax.dynamic_slice_in_dim(lon_reach, start, near, 0)
    offset = jnp.abs(lax.iota(jnp.int32, tap_count) - tap_count // 2)
    table = jnp.where((offset[None, :] <= reach[:, None])[None, :, None, :], table, jnp.zeros_like(table))
    return jnp.transpose(table, (0, 2, 1, 3))


def prepare_kernel(off_ref, taps, f_ref, band, f_mid, f_edge, lines):
    basis_count, row_span, near, tap_count = taps.shape
    lat_dev = band.shape[0]
    half = row_span // 2
    wide = 2 * BLOCK
    tap = lax.broadcasted_iota(jnp.int32, (tap_count, 128), 0)
    lane = lax.broadcasted_iota(jnp.int32, (tap_count, 128), 1)
    lines[...] = jnp.zeros_like(lines)
    for s in range(row_span):
        turn = (lane == s % 2 * wide + tap_count - 1 - tap).astype(bf16)
        for k in range(basis_count):
            lines[k, s, 8 : 8 + near, :] = jnp.dot(taps[k, s], turn, preferred_element_type=f32)
    off = off_ref[0] + 8 + 2 * half
    for k in range(basis_count):
        for p in range((row_span + 1) // 2):
            pair = lines[k, 2 * p, pl.ds(off - 2 * p, lat_dev), :]
            if 2 * p + 1 < row_span:
                pair = pair + lines[k, 2 * p + 1, pl.ds(off - 2 * p - 1, lat_dev), :]
            for i in range(lat_dev):
                line = jnp.broadcast_to(pair[i : i + 1, :], (BLOCK, 128))
                line = pltpu.roll(line, 0, 1, stride=1, stride_axis=0)
                band[i, k * BLOCK : (k + 1) * BLOCK, p * 128 : (p + 1) * 128] = line.astype(bf16)
    lane = lax.broadcasted_iota(jnp.int32, (1, 128), 1)
    for i in range(0, lat_dev, 2):
        even = f_ref[:, i * 128 : (i + 1) * 128].astype(f32)
        odd = f_ref[:, (i + 1) * 128 : (i + 2) * 128].astype(f32)
        back = lambda x: pltpu.roll(x, 128 - BLOCK, 1)
        ahead = lambda x: pltpu.roll(x, BLOCK, 1)
        at = slice(i * wide, (i + 2) * wide)
        f_mid[:, at] = jnp.where(lane < wide, back(even), ahead(odd)).astype(bf16)
        f_edge[:, at] = jnp.where(lane < wide, ahead(even), back(odd)).astype(bf16)


def rim_kernel(main, up, down, tail, head):
    half, lat_dev, side = up.shape[0], main.shape[0], tail.shape[1]
    last = main.shape[1] - side
    tail[:half] = up[:, last:, :]
    tail[half : half + lat_dev] = main[:, last:, :]
    tail[half + lat_dev :] = down[:, last:, :]
    head[:half] = up[:, :side, :]
    head[half : half + lat_dev] = main[:, :side, :]
    head[half + lat_dev :] = down[:, :side, :]


def convolve(band, ext, place, q_ref):
    basis_count, lat_dev, columns, _ = q_ref.shape
    row_span = ext.shape[0] - lat_dev + 1
    for i in range(lat_dev):
        for j in range(columns // BLOCK):
            parts = [ext[(i + row_span - 1 - s,) + place(j)] for s in range(row_span)]
            window = jnp.concatenate(parts + [jnp.zeros_like(parts[0])], axis=0)
            out = jnp.dot(band[i], window, preferred_element_type=f32).astype(bf16)
            for k in range(basis_count):
                q_ref[k, i, j * BLOCK : (j + 1) * BLOCK, :] = out[k * BLOCK : (k + 1) * BLOCK, :]


def middle_kernel(band, main, up, down, f_ref, q_ref, total, ext):
    lat_dev, half = main.shape[0], up.shape[0]
    ext[:half] = up[...]
    ext[half : half + lat_dev] = main[...]
    ext[half + lat_dev :] = down[...]
    side = BLOCK // 2
    convolve(band, ext, lambda j: (slice(side + j * BLOCK, side + (j + 2) * BLOCK),), q_ref)
    for k in range(q_ref.shape[0]):
        cells = q_ref[k].reshape(f_ref.shape[1], q_ref.shape[3])
        total[k] = jnp.dot(f_ref[...], cells, preferred_element_type=f32)


def edge_kernel(band, main, up, down, left, right, f_ref, total, q_ref, low, high, ext):
    lat_dev, lon_dev, channels = main.shape
    half, side = up.shape[0], left.shape[1]
    inner = 2 * BLOCK - side
    for first, last, source in ((0, half, up), (half, half + lat_dev, main), (half + lat_dev, 2 * half + lat_dev, down)):
        ext[first:last, 0, :inner, :] = source[:, lon_dev - inner :, :]
        ext[first:last, 1, side:, :] = source[:, :inner, :]
    ext[:, 0, inner:, :] = right[...]
    ext[:, 1, :side, :] = left[...]
    convolve(band, ext, lambda j: (j,), q_ref)
    for k in range(q_ref.shape[0]):
        cells = q_ref[k].reshape(f_ref.shape[1], channels)
        out = total[k] + jnp.dot(f_ref[...], cells, preferred_element_type=f32)
        low[k] = out[:, : channels // 2]
        high[k] = out[:, channels // 2 :]


def call(kernel, out_shape, operands, scratch=(), scalars=0, flops=10**9, mib=16):
    vmem = pl.BlockSpec(memory_space=pltpu.VMEM)
    smem = pl.BlockSpec(memory_space=pltpu.SMEM)
    return pl.pallas_call(
        kernel,
        out_shape=out_shape,
        in_specs=[smem] * scalars + [vmem] * (len(operands) - scalars),
        out_specs=jax.tree.map(lambda _: vmem, out_shape),
        scratch_shapes=list(scratch),
        compiler_params=pltpu.CompilerParams(vmem_limit_bytes=mib * 1024 * 1024),
        cost_estimate=pl.CostEstimate(flops=flops, bytes_accessed=10**6, transcendentals=0),
    )(*operands)


def mix_kernel(w_ref, mid_ref, edge_ref, out_ref):
    basis_count, lat_dev, columns, channels = mid_ref.shape
    for i in range(0, lat_dev, 2):
        total = jnp.zeros((channels, 4 * columns), f32)
        for k in range(basis_count):
            parts = []
            for row in (i, i + 1):
                parts += [edge_ref[k, row, BLOCK:], mid_ref[k, row], edge_ref[k, row, :BLOCK]]
            total += lax.dot_general(
                w_ref[k], jnp.concatenate(parts, axis=0), (((1,), (1,)), ((), ())), preferred_element_type=f32
            )
        out_ref[:, i * 2 * columns : (i + 2) * 2 * columns] = total.astype(bf16)


def all_to_all(x, axes):
    return lax.all_to_all(x, axes, 0, 0, tiled=True)


def to_all(x, count):
    return jnp.broadcast_to(x[None], (count,) + x.shape)


def reduce_all(low, high, core, scale, beside):
    swap = [(0, 1), (1, 0)]
    basis_count, channels, half = low.shape
    plane = 1
    for axis in PLANE:
        plane *= lax.axis_size(axis)
    depth = lax.axis_size("z")
    keep, send = jnp.where(core == 0, low, high), jnp.where(core == 0, high, low)
    came, beside = lax.optimization_barrier((lax.ppermute(send, "core", swap), beside))
    own = keep + came
    own = own.reshape(plane, -1, half).astype(bf16)
    own = jnp.sum(all_to_all(own, PLANE).astype(f32), axis=0).astype(bf16)
    own = jnp.sum(all_to_all(to_all(own, depth), ("z",)).astype(f32), axis=0)
    own = (own * scale).astype(bf16)
    own = all_to_all(to_all(own, plane), PLANE).reshape(basis_count, channels, half)
    other = lax.ppermute(own, "core", swap)
    low, high = jnp.where(core == 0, own, other), jnp.where(core == 0, other, own)
    return jnp.concatenate([low, high], axis=2).astype(f32), beside


def local(fields, grad_out, weight, basis_table, lon_reach):
    channels, lat_dev, lon_dev = fields.shape
    basis_count, nlat_all, row_span, tap_count = basis_table.shape
    half, side = row_span // 2, tap_count // 2
    near, wide = lat_dev + 2 * half, 2 * BLOCK
    shape = jax.ShapeDtypeStruct
    core = lax.axis_index("core")
    main = jnp.transpose(grad_out, (1, 2, 0))
    up = shift(main[lat_dev - half :], LAT, 1, False)
    down = shift(main[:half], LAT, -1, False)
    rim = shape((near, side, channels), bf16)
    tail, head = call(rim_kernel, (rim, rim), (main, up, down), flops=10**6, mib=4)
    left = shift(tail, LON, 1, True)
    right = shift(head, LON, -1, True)
    above = lax.axis_index(LAT) * lat_dev - half
    held = min(16, nlat_all)
    start = jnp.clip(above, 0, nlat_all - held)
    taps = tap_rows(basis_table, lon_reach, start, held)
    band, f_mid, f_edge = call(
        prepare_kernel,
        (
            shape((lat_dev, basis_count * BLOCK, (row_span + 1) * wide), bf16),
            shape((channels, lat_dev * wide), bf16),
            shape((channels, lat_dev * wide), bf16),
        ),
        ((above - start)[None], taps, fields.reshape(channels, lat_dev * lon_dev)),
        [pltpu.VMEM((basis_count, row_span, held + 16, 128), f32)],
        scalars=1,
        mib=12,
    )
    q_shape = shape((basis_count, lat_dev, wide, channels), bf16)
    part = shape((basis_count, channels, channels // 2), f32)
    q_mid, total = call(
        middle_kernel,
        (q_shape, shape((basis_count, channels, channels), f32)),
        (band, main, up, down, f_mid),
        [pltpu.VMEM((near, lon_dev, channels), bf16)],
    )
    q_edge, low, high = call(
        edge_kernel,
        (q_shape, part, part),
        (band, main, up, down, left, right, f_edge, total),
        [pltpu.VMEM((near, 2, wide, channels), bf16)],
    )
    mixed = call(mix_kernel, shape((channels, lat_dev * lon_dev), bf16), (weight, q_mid, q_edge))
    field_grad = mixed.reshape(channels, lat_dev, lon_dev)
    weight_grad, field_grad = reduce_all(low, high, core, 1.0 / nlat_all, field_grad)
    return field_grad, weight_grad


def solution(mesh):
    fine = Mesh(mesh.devices.reshape(4, 2, 2, 8, 2), ("y", "x_lo", "core", "z", "x_hi"))
    split = P(None, LAT, LON)
    return jax.shard_map(
        local,
        mesh=fine,
        in_specs=(split, split, P(), P(), P()),
        out_specs=(split, P()),
        check_vma=False,
    )
```

```python
import jax
import jax.numpy as jnp
from jax import lax
from jax.experimental import pallas as pl
from jax.experimental.pallas import tpu as pltpu
from jax.sharding import Mesh, PartitionSpec as P

LAT = ("y", "x_lo", "core")
LON = ("z", "x_hi")
PLANE = ("y", "x_hi", "x_lo")
BLOCK = 32
bf16, f32 = jnp.bfloat16, jnp.float32


def exchange(to_next, to_before, axes, closed):
    count = 1
    for axis in axes:
        count *= lax.axis_size(axis)
    even = lax.axis_index(axes[-1]) % 2 == 0
    near = [(i, i ^ 1) for i in range(count)]
    far = [(i, (i + 1 - 2 * (i % 2 == 0)) % count) for i in range(count)]
    if not closed:
        far = far[1:-1]
    came_near = lax.ppermute(jnp.where(even, to_next, to_before), axes, near)
    came_far = lax.ppermute(jnp.where(even, to_before, to_next), axes, far)
    return jnp.where(even, came_far, came_near), jnp.where(even, came_near, came_far)


def tap_rows(basis_table, lon_reach, start, near):
    tap_count = basis_table.shape[3]
    table = lax.dynamic_slice_in_dim(basis_table, start, near, 1)
    reach = lax.dynamic_slice_in_dim(lon_reach, start, near, 0)
    offset = jnp.abs(lax.iota(jnp.int32, tap_count) - tap_count // 2)
    table = jnp.where((offset[None, :] <= reach[:, None])[None, :, None, :], table, jnp.zeros_like(table))
    return jnp.transpose(table, (0, 2, 1, 3))


def prepare_kernel(off_ref, taps, f_ref, band, f_mid, f_edge, lines):
    basis_count, row_span, near, tap_count = taps.shape
    lat_dev = band.shape[0]
    half = row_span // 2
    wide = 2 * BLOCK
    tap = lax.broadcasted_iota(jnp.int32, (tap_count, 128), 0)
    lane = lax.broadcasted_iota(jnp.int32, (tap_count, 128), 1)
    lines[...] = jnp.zeros_like(lines)
    for s in range(row_span):
        turn = (lane == s % 2 * wide + tap_count - 1 - tap).astype(bf16)
        for k in range(basis_count):
            lines[k, s, 8 : 8 + near, :] = jnp.dot(taps[k, s], turn, preferred_element_type=f32)
    off = off_ref[0] + 8 + 2 * half
    for k in range(basis_count):
        for p in range((row_span + 1) // 2):
            pair = lines[k, 2 * p, pl.ds(off - 2 * p, lat_dev), :]
            if 2 * p + 1 < row_span:
                pair = pair + lines[k, 2 * p + 1, pl.ds(off - 2 * p - 1, lat_dev), :]
            for i in range(lat_dev):
                line = jnp.broadcast_to(pair[i : i + 1, :], (BLOCK, 128))
                line = pltpu.roll(line, 0, 1, stride=1, stride_axis=0)
                band[i, k * BLOCK : (k + 1) * BLOCK, p * 128 : (p + 1) * 128] = line.astype(bf16)
    lane = lax.broadcasted_iota(jnp.int32, (1, 128), 1)
    for i in range(0, lat_dev, 2):
        even = f_ref[:, i * 128 : (i + 1) * 128].astype(f32)
        odd = f_ref[:, (i + 1) * 128 : (i + 2) * 128].astype(f32)
        back = lambda x: pltpu.roll(x, 128 - BLOCK, 1)
        ahead = lambda x: pltpu.roll(x, BLOCK, 1)
        at = slice(i * wide, (i + 2) * wide)
        f_mid[:, at] = jnp.where(lane < wide, back(even), ahead(odd)).astype(bf16)
        f_edge[:, at] = jnp.where(lane < wide, ahead(even), back(odd)).astype(bf16)


def rim_kernel(main, up, down, tail, head):
    half, lat_dev, side = up.shape[0], main.shape[0], tail.shape[1]
    last = main.shape[1] - side
    tail[:half] = up[:, last:, :]
    tail[half : half + lat_dev] = main[:, last:, :]
    tail[half + lat_dev :] = down[:, last:, :]
    head[:half] = up[:, :side, :]
    head[half : half + lat_dev] = main[:, :side, :]
    head[half + lat_dev :] = down[:, :side, :]


def convolve(band, ext, place, q_ref):
    basis_count, lat_dev, columns, _ = q_ref.shape
    row_span = ext.shape[0] - lat_dev + 1
    for i in range(lat_dev):
        for j in range(columns // BLOCK):
            parts = [ext[(i + row_span - 1 - s,) + place(j)] for s in range(row_span)]
            window = jnp.concatenate(parts + [jnp.zeros_like(parts[0])], axis=0)
            out = jnp.dot(band[i], window, preferred_element_type=f32).astype(bf16)
            for k in range(basis_count):
                q_ref[k, i, j * BLOCK : (j + 1) * BLOCK, :] = out[k * BLOCK : (k + 1) * BLOCK, :]


def middle_kernel(band, main, up, down, f_ref, q_ref, total, ext):
    lat_dev, half = main.shape[0], up.shape[0]
    ext[:half] = up[...]
    ext[half : half + lat_dev] = main[...]
    ext[half + lat_dev :] = down[...]
    side = BLOCK // 2
    convolve(band, ext, lambda j: (slice(side + j * BLOCK, side + (j + 2) * BLOCK),), q_ref)
    for k in range(q_ref.shape[0]):
        cells = q_ref[k].reshape(f_ref.shape[1], q_ref.shape[3])
        total[k] = jnp.dot(f_ref[...], cells, preferred_element_type=f32)


def edge_kernel(band, main, up, down, left, right, f_ref, total, q_ref, low, high, ext):
    lat_dev, lon_dev, channels = main.shape
    half, side = up.shape[0], left.shape[1]
    inner = 2 * BLOCK - side
    for first, last, source in ((0, half, up), (half, half + lat_dev, main), (half + lat_dev, 2 * half + lat_dev, down)):
        ext[first:last, 0, :inner, :] = source[:, lon_dev - inner :, :]
        ext[first:last, 1, side:, :] = source[:, :inner, :]
    ext[:, 0, inner:, :] = right[...]
    ext[:, 1, :side, :] = left[...]
    convolve(band, ext, lambda j: (j,), q_ref)
    for k in range(q_ref.shape[0]):
        cells = q_ref[k].reshape(f_ref.shape[1], channels)
        out = total[k] + jnp.dot(f_ref[...], cells, preferred_element_type=f32)
        low[k] = out[:, : channels // 2]
        high[k] = out[:, channels // 2 :]


def call(kernel, out_shape, operands, scratch=(), scalars=0, flops=10**9, mib=16):
    vmem = pl.BlockSpec(memory_space=pltpu.VMEM)
    smem = pl.BlockSpec(memory_space=pltpu.SMEM)
    return pl.pallas_call(
        kernel,
        out_shape=out_shape,
        in_specs=[smem] * scalars + [vmem] * (len(operands) - scalars),
        out_specs=jax.tree.map(lambda _: vmem, out_shape),
        scratch_shapes=list(scratch),
        compiler_params=pltpu.CompilerParams(vmem_limit_bytes=mib * 1024 * 1024),
        cost_estimate=pl.CostEstimate(flops=flops, bytes_accessed=10**6, transcendentals=0),
    )(*operands)


def mix_kernel(w_ref, mid_ref, edge_ref, out_ref):
    basis_count, lat_dev, columns, channels = mid_ref.shape
    for i in range(0, lat_dev, 2):
        total = jnp.zeros((channels, 4 * columns), f32)
        for k in range(basis_count):
            parts = []
            for row in (i, i + 1):
                parts += [edge_ref[k, row, BLOCK:], mid_ref[k, row], edge_ref[k, row, :BLOCK]]
            total += lax.dot_general(
                w_ref[k], jnp.concatenate(parts, axis=0), (((1,), (1,)), ((), ())), preferred_element_type=f32
            )
        out_ref[:, i * 2 * columns : (i + 2) * 2 * columns] = total.astype(bf16)


def all_to_all(x, axes):
    return lax.all_to_all(x, axes, 0, 0, tiled=True)


def to_all(x, count):
    return jnp.broadcast_to(x[None], (count,) + x.shape)


def reduce_all(low, high, core, scale, beside):
    swap = [(0, 1), (1, 0)]
    basis_count, channels, half = low.shape
    plane = 1
    for axis in PLANE:
        plane *= lax.axis_size(axis)
    depth = lax.axis_size("z")
    keep, send = jnp.where(core == 0, low, high), jnp.where(core == 0, high, low)
    came, beside = lax.optimization_barrier((lax.ppermute(send, "core", swap), beside))
    own = keep + came
    own = own.reshape(plane, -1, half).astype(bf16)
    own = jnp.sum(all_to_all(own, PLANE).astype(f32), axis=0).astype(bf16)
    own = jnp.sum(all_to_all(to_all(own, depth), ("z",)).astype(f32), axis=0)
    own = (own * scale).astype(bf16)
    own = all_to_all(to_all(own, plane), PLANE).reshape(basis_count, channels, half)
    other = lax.ppermute(own, "core", swap)
    low, high = jnp.where(core == 0, own, other), jnp.where(core == 0, other, own)
    return jnp.concatenate([low, high], axis=2).astype(f32), beside


def local(fields, grad_out, weight, basis_table, lon_reach):
    channels, lat_dev, lon_dev = fields.shape
    basis_count, nlat_all, row_span, tap_count = basis_table.shape
    half, side = row_span // 2, tap_count // 2
    near, wide = lat_dev + 2 * half, 2 * BLOCK
    shape = jax.ShapeDtypeStruct
    core = lax.axis_index("core")
    main = jnp.transpose(grad_out, (1, 2, 0))
    up, down = exchange(main[lat_dev - half :], main[:half], LAT, False)
    rim = shape((near, side, channels), bf16)
    tail, head = call(rim_kernel, (rim, rim), (main, up, down), flops=10**6, mib=4)
    left, right = exchange(tail, head, LON, True)
    above = lax.axis_index(LAT) * lat_dev - half
    held = min(16, nlat_all)
    start = jnp.clip(above, 0, nlat_all - held)
    taps = tap_rows(basis_table, lon_reach, start, held)
    band, f_mid, f_edge = call(
        prepare_kernel,
        (
            shape((lat_dev, basis_count * BLOCK, (row_span + 1) * wide), bf16),
            shape((channels, lat_dev * wide), bf16),
            shape((channels, lat_dev * wide), bf16),
        ),
        ((above - start)[None], taps, fields.reshape(channels, lat_dev * lon_dev)),
        [pltpu.VMEM((basis_count, row_span, held + 16, 128), f32)],
        scalars=1,
        mib=12,
    )
    q_shape = shape((basis_count, lat_dev, wide, channels), bf16)
    part = shape((basis_count, channels, channels // 2), f32)
    q_mid, total = call(
        middle_kernel,
        (q_shape, shape((basis_count, channels, channels), f32)),
        (band, main, up, down, f_mid),
        [pltpu.VMEM((near, lon_dev, channels), bf16)],
    )
    q_edge, low, high = call(
        edge_kernel,
        (q_shape, part, part),
        (band, main, up, down, left, right, f_edge, total),
        [pltpu.VMEM((near, 2, wide, channels), bf16)],
    )
    mixed = call(mix_kernel, shape((channels, lat_dev * lon_dev), bf16), (weight, q_mid, q_edge))
    field_grad = mixed.reshape(channels, lat_dev, lon_dev)
    weight_grad, field_grad = reduce_all(low, high, core, 1.0 / nlat_all, field_grad)
    return field_grad, weight_grad


def solution(mesh):
    fine = Mesh(mesh.devices.reshape(4, 2, 2, 8, 2), ("y", "x_lo", "core", "z", "x_hi"))
    split = P(None, LAT, LON)
    return jax.shard_map(
        local,
        mesh=fine,
        in_specs=(split, split, P(), P(), P()),
        out_specs=(split, P()),
        check_vma=False,
    )
```

```python
import jax
import jax.numpy as jnp
from jax import lax
from jax.experimental import pallas as pl
from jax.experimental.pallas import tpu as pltpu
from jax.sharding import Mesh, PartitionSpec as P

LAT = ("y", "x_lo", "core")
LON = ("z", "x_hi")
PLANE = ("y", "x_hi", "x_lo")
BLOCK = 32
bf16, f32 = jnp.bfloat16, jnp.float32


def exchange(first, second, axes, closed):
    count = 1
    for axis in axes:
        count *= lax.axis_size(axis)
    near = [(i, i ^ 1) for i in range(count)]
    far = [(i, (i + 1 - 2 * (i % 2 == 0)) % count) for i in range(count)]
    if not closed:
        far = far[1:-1]
    return lax.ppermute(first, axes, near), lax.ppermute(second, axes, far)


def tap_rows(basis_table, lon_reach, start, near):
    tap_count = basis_table.shape[3]
    table = lax.dynamic_slice_in_dim(basis_table, start, near, 1)
    reach = lax.dynamic_slice_in_dim(lon_reach, start, near, 0)
    offset = jnp.abs(lax.iota(jnp.int32, tap_count) - tap_count // 2)
    table = jnp.where((offset[None, :] <= reach[:, None])[None, :, None, :], table, jnp.zeros_like(table))
    return jnp.transpose(table, (0, 2, 1, 3))


def rim_kernel(flags, main, near, far, first, second):
    lat_dev, lon_dev, _ = main.shape
    half, side = near.shape[0], first.shape[1]
    for even in (0, 1):
        last = lon_dev - side

        @pl.when(flags[2] == even)
        def _():
            for ref, at in ((first, last if even else 0), (second, 0 if even else last)):
                ref[half : half + lat_dev] = main[:, at : at + side, :]
                for upper in (0, 1):

                    @pl.when(flags[1] == upper)
                    def _():
                        up, down = (far, near) if upper else (near, far)
                        ref[:half] = up[:, at : at + side, :]
                        ref[half + lat_dev :] = down[:, at : at + side, :]


def convolve(band, ext, place, q_ref):
    basis_count, lat_dev, columns, _ = q_ref.shape
    row_span = ext.shape[0] - lat_dev + 1
    for i in range(lat_dev):
        for j in range(columns // BLOCK):
            parts = [ext[(i + row_span - 1 - s,) + place(j)] for s in range(row_span)]
            window = jnp.concatenate(parts + [jnp.zeros_like(parts[0])], axis=0)
            out = jnp.dot(band[i], window, preferred_element_type=f32).astype(bf16)
            for k in range(basis_count):
                q_ref[k, i, j * BLOCK : (j + 1) * BLOCK, :] = out[k * BLOCK : (k + 1) * BLOCK, :]


def build_band(off, taps, band, lines):
    basis_count, row_span, near, tap_count = taps.shape
    lat_dev = band.shape[0]
    wide = 2 * BLOCK
    tap = lax.broadcasted_iota(jnp.int32, (tap_count, 128), 0)
    lane = lax.broadcasted_iota(jnp.int32, (tap_count, 128), 1)
    lines[...] = jnp.zeros_like(lines)
    for s in range(row_span):
        turn = (lane == s % 2 * wide + tap_count - 1 - tap).astype(bf16)
        for k in range(basis_count):
            lines[k, s, 8 : 8 + near, :] = jnp.dot(taps[k, s], turn, preferred_element_type=f32)
    base = off + 8 + row_span - 1
    for k in range(basis_count):
        for p in range((row_span + 1) // 2):
            pair = lines[k, 2 * p, pl.ds(base - 2 * p, lat_dev), :]
            if 2 * p + 1 < row_span:
                pair = pair + lines[k, 2 * p + 1, pl.ds(base - 2 * p - 1, lat_dev), :]
            for i in range(lat_dev):
                line = jnp.broadcast_to(pair[i : i + 1, :], (BLOCK, 128))
                line = pltpu.roll(line, 0, 1, stride=1, stride_axis=0)
                band[i, k * BLOCK : (k + 1) * BLOCK, p * 128 : (p + 1) * 128] = line.astype(bf16)


def cut_fields(f_ref, f_mid, f_edge):
    wide = 2 * BLOCK
    lane = lax.broadcasted_iota(jnp.int32, (1, 128), 1)
    for i in range(0, f_ref.shape[1] // 128, 2):
        even = f_ref[:, i * 128 : (i + 1) * 128].astype(f32)
        odd = f_ref[:, (i + 1) * 128 : (i + 2) * 128].astype(f32)
        back = lambda x: pltpu.roll(x, 128 - BLOCK, 1)
        ahead = lambda x: pltpu.roll(x, BLOCK, 1)
        at = slice(i * wide, (i + 2) * wide)
        f_mid[:, at] = jnp.where(lane < wide, back(even), ahead(odd)).astype(bf16)
        f_edge[:, at] = jnp.where(lane < wide, ahead(even), back(odd)).astype(bf16)


def middle_kernel(flags, taps, f_ref, main, near, far, band, f_edge, q_ref, total, window, lines, f_mid, ext):
    lat_dev, lon_dev, channels = main.shape
    half, side = near.shape[0], BLOCK // 2
    inner = window.shape[2]
    build_band(flags[0], taps, band, lines)
    cut_fields(f_ref, f_mid, f_edge)
    ext[half : half + lat_dev] = main[...]
    for upper in (0, 1):

        @pl.when(flags[1] == upper)
        def _():
            ext[:half] = (far if upper else near)[...]
            ext[half + lat_dev :] = (near if upper else far)[...]

    window[:, 0] = ext[:, lon_dev - inner :, :]
    window[:, 1] = ext[:, :inner, :]
    convolve(band, ext, lambda j: (slice(side + j * BLOCK, side + (j + 2) * BLOCK),), q_ref)
    for k in range(q_ref.shape[0]):
        cells = q_ref[k].reshape(f_mid.shape[1], channels)
        total[k] = jnp.dot(f_mid[...], cells, preferred_element_type=f32)


def edge_kernel(flags, band, window, near, far, f_ref, total, q_ref, low, high, ext):
    channels = window.shape[3]
    side, inner = near.shape[1], window.shape[2]
    ext[:, 0, :inner, :] = window[:, 0]
    ext[:, 1, side:, :] = window[:, 1]
    for even in (0, 1):

        @pl.when(flags[2] == even)
        def _():
            ext[:, 0, inner:, :] = (near if even else far)[...]
            ext[:, 1, :side, :] = (far if even else near)[...]

    convolve(band, ext, lambda j: (j,), q_ref)
    for k in range(q_ref.shape[0]):
        cells = q_ref[k].reshape(f_ref.shape[1], channels)
        out = total[k] + jnp.dot(f_ref[...], cells, preferred_element_type=f32)
        low[k] = out[:, : channels // 2]
        high[k] = out[:, channels // 2 :]


def call(kernel, out_shape, operands, scratch=(), scalars=0, flops=10**9, mib=16):
    vmem = pl.BlockSpec(memory_space=pltpu.VMEM)
    smem = pl.BlockSpec(memory_space=pltpu.SMEM)
    return pl.pallas_call(
        kernel,
        out_shape=out_shape,
        in_specs=[smem] * scalars + [vmem] * (len(operands) - scalars),
        out_specs=jax.tree.map(lambda _: vmem, out_shape),
        scratch_shapes=list(scratch),
        compiler_params=pltpu.CompilerParams(vmem_limit_bytes=mib * 1024 * 1024),
        cost_estimate=pl.CostEstimate(flops=flops, bytes_accessed=10**6, transcendentals=0),
    )(*operands)


def mix_kernel(w_ref, mid_ref, edge_ref, out_ref):
    basis_count, lat_dev, columns, channels = mid_ref.shape
    for i in range(0, lat_dev, 2):
        total = jnp.zeros((channels, 4 * columns), f32)
        for k in range(basis_count):
            parts = []
            for row in (i, i + 1):
                parts += [edge_ref[k, row, BLOCK:], mid_ref[k, row], edge_ref[k, row, :BLOCK]]
            total += lax.dot_general(
                w_ref[k], jnp.concatenate(parts, axis=0), (((1,), (1,)), ((), ())), preferred_element_type=f32
            )
        out_ref[:, i * 2 * columns : (i + 2) * 2 * columns] = total.astype(bf16)


def all_to_all(x, axes):
    return lax.all_to_all(x, axes, 0, 0, tiled=True)


def to_all(x, count):
    return jnp.broadcast_to(x[None], (count,) + x.shape)


def reduce_all(low, high, core, scale, beside):
    swap = [(0, 1), (1, 0)]
    basis_count, channels, half = low.shape
    plane = 1
    for axis in PLANE:
        plane *= lax.axis_size(axis)
    depth = lax.axis_size("z")
    keep, send = jnp.where(core == 0, low, high), jnp.where(core == 0, high, low)
    came, beside = lax.optimization_barrier((lax.ppermute(send, "core", swap), beside))
    own = keep + came
    own = own.reshape(plane, -1, half).astype(bf16)
    own = jnp.sum(all_to_all(own, PLANE).astype(f32), axis=0).astype(bf16)
    own = jnp.sum(all_to_all(to_all(own, depth), ("z",)).astype(f32), axis=0)
    own = (own * scale).astype(bf16)
    own = all_to_all(to_all(own, plane), PLANE).reshape(basis_count, channels, half)
    other = lax.ppermute(own, "core", swap)
    low, high = jnp.where(core == 0, own, other), jnp.where(core == 0, other, own)
    return jnp.concatenate([low, high], axis=2).astype(f32), beside


def local(fields, grad_out, weight, basis_table, lon_reach):
    channels, lat_dev, lon_dev = fields.shape
    basis_count, nlat_all, row_span, tap_count = basis_table.shape
    half, side = row_span // 2, tap_count // 2
    near, wide = lat_dev + 2 * half, 2 * BLOCK
    shape = jax.ShapeDtypeStruct
    core = lax.axis_index("core")
    above = lax.axis_index(LAT) * lat_dev - half
    held = min(16, nlat_all)
    start = jnp.clip(above, 0, nlat_all - held)
    upper = core == 0
    even = lax.axis_index(LON) % 2 == 0
    flags = jnp.stack([above - start, upper.astype(jnp.int32), even.astype(jnp.int32)])
    main = jnp.transpose(grad_out, (1, 2, 0))
    last, first = main[lat_dev - half :], main[:half]
    near_lat, far_lat = exchange(jnp.where(upper, last, first), jnp.where(upper, first, last), LAT, False)
    rim = shape((near, side, channels), bf16)
    rims = call(rim_kernel, (rim, rim), (flags, main, near_lat, far_lat), scalars=1, flops=10**6, mib=4)
    near_lon, far_lon = exchange(*rims, LON, True)
    taps = tap_rows(basis_table, lon_reach, start, held)
    q_shape = shape((basis_count, lat_dev, wide, channels), bf16)
    columns = shape((channels, lat_dev * wide), bf16)
    part = shape((basis_count, channels, channels // 2), f32)
    band, f_edge, q_mid, total, window = call(
        middle_kernel,
        (
            shape((lat_dev, basis_count * BLOCK, (row_span + 1) * wide), bf16),
            columns,
            q_shape,
            shape((basis_count, channels, channels), f32),
            shape((near, 2, wide - side, channels), bf16),
        ),
        (flags, taps, fields.reshape(channels, lat_dev * lon_dev), main, near_lat, far_lat),
        [
            pltpu.VMEM((basis_count, row_span, held + 16, 128), f32),
            pltpu.VMEM(columns.shape, bf16),
            pltpu.VMEM((near, lon_dev, channels), bf16),
        ],
        scalars=1,
    )
    q_edge, low, high = call(
        edge_kernel,
        (q_shape, part, part),
        (flags, band, window, near_lon, far_lon, f_edge, total),
        [pltpu.VMEM((near, 2, wide, channels), bf16)],
        scalars=1,
    )
    mixed = call(mix_kernel, shape((channels, lat_dev * lon_dev), bf16), (weight, q_mid, q_edge))
    field_grad = mixed.reshape(channels, lat_dev, lon_dev)
    weight_grad, field_grad = reduce_all(low, high, core, 1.0 / nlat_all, field_grad)
    return field_grad, weight_grad


def solution(mesh):
    fine = Mesh(mesh.devices.reshape(4, 2, 2, 8, 2), ("y", "x_lo", "core", "z", "x_hi"))
    split = P(None, LAT, LON)
    return jax.shard_map(
        local,
        mesh=fine,
        in_specs=(split, split, P(), P(), P()),
        out_specs=(split, P()),
        check_vma=False,
    )
```

```python
import functools

import jax
import jax.numpy as jnp
from jax import lax
from jax.experimental import pallas as pl
from jax.experimental.pallas import tpu as pltpu
from jax.sharding import Mesh, PartitionSpec as P

LAT = ("y", "x_lo", "core")
LON = ("z", "x_hi")
PLANE = ("y", "x_hi", "x_lo")
BLOCK = 32
bf16, f32 = jnp.bfloat16, jnp.float32


def exchange(first, second, axes, closed):
    count = 1
    for axis in axes:
        count *= lax.axis_size(axis)
    near = [(i, i ^ 1) for i in range(count)]
    far = [(i, (i + 1 - 2 * (i % 2 == 0)) % count) for i in range(count)]
    if not closed:
        far = far[1:-1]
    return lax.ppermute(first, axes, near), lax.ppermute(second, axes, far)


def parity(axes):
    return lax.rem(lax.axis_index(axes[-1]), 2)


def held_rows(lat_dev, half, nlat_all):
    above = lax.axis_index(LAT) * lat_dev - half
    held = min(16, nlat_all)
    return above, jnp.clip(above, 0, nlat_all - held), held


def tap_rows(basis_table, lon_reach, start, near):
    tap_count = basis_table.shape[3]
    table = lax.dynamic_slice_in_dim(basis_table, start, near, 1)
    reach = lax.dynamic_slice_in_dim(lon_reach, start, near, 0)
    offset = jnp.abs(lax.iota(jnp.int32, tap_count) - tap_count // 2)
    table = jnp.where((offset[None, :] <= reach[:, None])[None, :, None, :], table, jnp.zeros_like(table))
    return jnp.transpose(table, (0, 2, 1, 3))


def rim_kernel(main, near, far, first, second):
    lat_dev, lon_dev, _ = main.shape
    half, side = near.shape[0], first.shape[1]
    odd_lon, odd_lat = parity(LON), parity(LAT)
    for even in (0, 1):
        last = lon_dev - side

        @pl.when(odd_lon != even)
        def _():
            for ref, at in ((first, last if even else 0), (second, 0 if even else last)):
                ref[half : half + lat_dev] = main[:, at : at + side, :]
                for upper in (0, 1):

                    @pl.when(odd_lat != upper)
                    def _():
                        up, down = (far, near) if upper else (near, far)
                        ref[:half] = up[:, at : at + side, :]
                        ref[half + lat_dev :] = down[:, at : at + side, :]


def convolve(band, ext, place, q_ref):
    basis_count, lat_dev, columns, _ = q_ref.shape
    row_span = ext.shape[0] - lat_dev + 1
    for i in range(lat_dev):
        for j in range(columns // BLOCK):
            parts = [ext[(i + row_span - 1 - s,) + place(j)] for s in range(row_span)]
            window = jnp.concatenate(parts + [jnp.zeros_like(parts[0])], axis=0)
            out = jnp.dot(band[i], window, preferred_element_type=f32).astype(bf16)
            for k in range(basis_count):
                q_ref[k, i, j * BLOCK : (j + 1) * BLOCK, :] = out[k * BLOCK : (k + 1) * BLOCK, :]


def build_band(off, taps, band, lines):
    basis_count, row_span, near, tap_count = taps.shape
    lat_dev = band.shape[0]
    wide = 2 * BLOCK
    tap = lax.broadcasted_iota(jnp.int32, (tap_count, 128), 0)
    lane = lax.broadcasted_iota(jnp.int32, (tap_count, 128), 1)
    lines[...] = jnp.zeros_like(lines)
    for s in range(row_span):
        turn = (lane == s % 2 * wide + tap_count - 1 - tap).astype(bf16)
        for k in range(basis_count):
            lines[k, s, 8 : 8 + near, :] = jnp.dot(taps[k, s], turn, preferred_element_type=f32)
    base = off + 8 + row_span - 1
    for k in range(basis_count):
        for p in range((row_span + 1) // 2):
            pair = lines[k, 2 * p, pl.ds(base - 2 * p, lat_dev), :]
            if 2 * p + 1 < row_span:
                pair = pair + lines[k, 2 * p + 1, pl.ds(base - 2 * p - 1, lat_dev), :]
            for i in range(lat_dev):
                line = jnp.broadcast_to(pair[i : i + 1, :], (BLOCK, 128))
                line = pltpu.roll(line, 0, 1, stride=1, stride_axis=0)
                band[i, k * BLOCK : (k + 1) * BLOCK, p * 128 : (p + 1) * 128] = line.astype(bf16)


def cut_fields(f_ref, f_mid, f_edge):
    wide = 2 * BLOCK
    lane = lax.broadcasted_iota(jnp.int32, (1, 128), 1)
    for i in range(0, f_ref.shape[1] // 128, 2):
        even = f_ref[:, i * 128 : (i + 1) * 128].astype(f32)
        odd = f_ref[:, (i + 1) * 128 : (i + 2) * 128].astype(f32)
        back = lambda x: pltpu.roll(x, 128 - BLOCK, 1)
        ahead = lambda x: pltpu.roll(x, BLOCK, 1)
        at = slice(i * wide, (i + 2) * wide)
        f_mid[:, at] = jnp.where(lane < wide, back(even), ahead(odd)).astype(bf16)
        f_edge[:, at] = jnp.where(lane < wide, ahead(even), back(odd)).astype(bf16)


def middle_kernel(nlat_all, taps, f_ref, main, near, far, band, f_edge, q_ref, total, window, lines, f_mid, ext):
    lat_dev, lon_dev, channels = main.shape
    half, side = near.shape[0], BLOCK // 2
    inner = window.shape[2]
    above, start, _ = held_rows(lat_dev, half, nlat_all)
    build_band(above - start, taps, band, lines)
    cut_fields(f_ref, f_mid, f_edge)
    ext[half : half + lat_dev] = main[...]
    odd_lat = parity(LAT)
    for upper in (0, 1):

        @pl.when(odd_lat != upper)
        def _():
            ext[:half] = (far if upper else near)[...]
            ext[half + lat_dev :] = (near if upper else far)[...]

    window[:, 0] = ext[:, lon_dev - inner :, :]
    window[:, 1] = ext[:, :inner, :]
    convolve(band, ext, lambda j: (slice(side + j * BLOCK, side + (j + 2) * BLOCK),), q_ref)
    for k in range(q_ref.shape[0]):
        cells = q_ref[k].reshape(f_mid.shape[1], channels)
        total[k] = jnp.dot(f_mid[...], cells, preferred_element_type=f32)


def edge_kernel(band, window, near, far, f_ref, total, w_ref, q_ref, low, high, w_out, ext, sem):
    fetch = pltpu.make_async_copy(w_ref, w_out, sem)
    fetch.start()
    channels = window.shape[3]
    side, inner = near.shape[1], window.shape[2]
    ext[:, 0, :inner, :] = window[:, 0]
    ext[:, 1, side:, :] = window[:, 1]
    odd_lon = parity(LON)
    for even in (0, 1):

        @pl.when(odd_lon != even)
        def _():
            ext[:, 0, inner:, :] = (near if even else far)[...]
            ext[:, 1, :side, :] = (far if even else near)[...]

    convolve(band, ext, lambda j: (j,), q_ref)
    for k in range(q_ref.shape[0]):
        cells = q_ref[k].reshape(f_ref.shape[1], channels)
        out = total[k] + jnp.dot(f_ref[...], cells, preferred_element_type=f32)
        low[k] = out[:, : channels // 2]
        high[k] = out[:, channels // 2 :]
    fetch.wait()


def call(kernel, out_shape, operands, scratch=(), hbm=0, flops=10**9, mib=16):
    vmem = pl.BlockSpec(memory_space=pltpu.VMEM)
    return pl.pallas_call(
        kernel,
        out_shape=out_shape,
        in_specs=[vmem] * (len(operands) - hbm) + [pl.BlockSpec(memory_space=pl.ANY)] * hbm,
        out_specs=jax.tree.map(lambda _: vmem, out_shape),
        scratch_shapes=list(scratch),
        compiler_params=pltpu.CompilerParams(vmem_limit_bytes=mib * 1024 * 1024),
        cost_estimate=pl.CostEstimate(flops=flops, bytes_accessed=10**6, transcendentals=0),
    )(*operands)


def mix_kernel(w_ref, mid_ref, edge_ref, out_ref):
    basis_count, lat_dev, columns, channels = mid_ref.shape
    for i in range(0, lat_dev, 2):
        total = jnp.zeros((channels, 4 * columns), f32)
        for k in range(basis_count):
            parts = []
            for row in (i, i + 1):
                parts += [edge_ref[k, row, BLOCK:], mid_ref[k, row], edge_ref[k, row, :BLOCK]]
            total += lax.dot_general(
                w_ref[k], jnp.concatenate(parts, axis=0), (((1,), (1,)), ((), ())), preferred_element_type=f32
            )
        out_ref[:, i * 2 * columns : (i + 2) * 2 * columns] = total.astype(bf16)


def place_kernel(own, half_ref, *refs):
    out, wide, sems = refs[-3:]
    basis_count, _, columns = half_ref.shape
    at = lax.axis_index("core") if own else 1 - lax.axis_index("core")
    at = pl.ds(pl.multiple_of(at * columns, columns), columns)
    parts = sems.shape[0]
    size = basis_count // parts
    copies = []
    for part in range(parts):
        rows = slice(part * size, (part + 1) * size)
        wide[rows] = half_ref[rows].astype(f32)
        copies.append(pltpu.make_async_copy(wide.at[rows], out.at[rows, :, at], sems.at[part]))
        copies[-1].start()
    for copy in copies:
        copy.wait()


def place(half, own, into=None):
    basis_count, channels, columns = half.shape
    hbm = pl.BlockSpec(memory_space=pl.ANY)
    operands = (half,) if into is None else (half, into)
    return pl.pallas_call(
        functools.partial(place_kernel, own),
        out_shape=jax.ShapeDtypeStruct((basis_count, channels, 2 * columns), f32),
        in_specs=[pl.BlockSpec(memory_space=pltpu.VMEM)] + [hbm] * (len(operands) - 1),
        out_specs=hbm,
        scratch_shapes=[pltpu.VMEM(half.shape, f32), pltpu.SemaphoreType.DMA((3,))],
        input_output_aliases={} if into is None else {1: 0},
        compiler_params=pltpu.CompilerParams(vmem_limit_bytes=4 * 1024 * 1024),
        cost_estimate=pl.CostEstimate(flops=10**6, bytes_accessed=10**6, transcendentals=0),
    )(*operands)


def all_to_all(x, axes):
    return lax.all_to_all(x, axes, 0, 0, tiled=True)


def to_all(x, count):
    return jnp.broadcast_to(x[None], (count,) + x.shape)


def reduce_all(low, high, core, scale, beside, finish):
    swap = [(0, 1), (1, 0)]
    basis_count, channels, half = low.shape
    plane = 1
    for axis in PLANE:
        plane *= lax.axis_size(axis)
    depth = lax.axis_size("z")
    keep, send = jnp.where(core == 0, low, high), jnp.where(core == 0, high, low)
    came, beside = lax.optimization_barrier((lax.ppermute(send, "core", swap), beside))
    own = keep + came
    own = own.reshape(plane, -1, half).astype(bf16)
    own = jnp.sum(all_to_all(own, PLANE).astype(f32), axis=0).astype(bf16)
    own = jnp.sum(all_to_all(to_all(own, depth), ("z",)).astype(f32), axis=0)
    own = (own * scale).astype(bf16)
    own = all_to_all(to_all(own, plane), PLANE).reshape(basis_count, channels, half)
    beside = finish(beside)
    other, summed, beside = lax.optimization_barrier((lax.ppermute(own, "core", swap), place(own, True), beside))
    return place(other, False, summed), beside


def local(fields, grad_out, weight, basis_table, lon_reach):
    channels, lat_dev, lon_dev = fields.shape
    basis_count, nlat_all, row_span, tap_count = basis_table.shape
    half, side = row_span // 2, tap_count // 2
    near, wide = lat_dev + 2 * half, 2 * BLOCK
    shape = jax.ShapeDtypeStruct
    core = lax.axis_index("core")
    _, start, held = held_rows(lat_dev, half, nlat_all)
    upper = core == 0
    main = jnp.transpose(grad_out, (1, 2, 0))
    last, first = main[lat_dev - half :], main[:half]
    near_lat, far_lat = exchange(jnp.where(upper, last, first), jnp.where(upper, first, last), LAT, False)
    rim = shape((near, side, channels), bf16)
    rims = call(rim_kernel, (rim, rim), (main, near_lat, far_lat), flops=10**6, mib=4)
    near_lon, far_lon = exchange(*rims, LON, True)
    taps = tap_rows(basis_table, lon_reach, start, held)
    q_shape = shape((basis_count, lat_dev, wide, channels), bf16)
    columns = shape((channels, lat_dev * wide), bf16)
    part = shape((basis_count, channels, channels // 2), f32)
    band, f_edge, q_mid, total, window = call(
        functools.partial(middle_kernel, nlat_all),
        (
            shape((lat_dev, basis_count * BLOCK, (row_span + 1) * wide), bf16),
            columns,
            q_shape,
            shape((basis_count, channels, channels), f32),
            shape((near, 2, wide - side, channels), bf16),
        ),
        (taps, fields.reshape(channels, lat_dev * lon_dev), main, near_lat, far_lat),
        [
            pltpu.VMEM((basis_count, row_span, held + 16, 128), f32),
            pltpu.VMEM(columns.shape, bf16),
            pltpu.VMEM((near, lon_dev, channels), bf16),
        ],
    )
    q_edge, low, high, weight = call(
        edge_kernel,
        (q_shape, part, part, shape(weight.shape, bf16)),
        (band, window, near_lon, far_lon, f_edge, total, weight),
        [pltpu.VMEM((near, 2, wide, channels), bf16), pltpu.SemaphoreType.DMA],
        hbm=1,
    )
    mixed = call(mix_kernel, shape((channels, lat_dev * lon_dev), bf16), (weight, q_mid, q_edge))
    weight_grad, field_grad = reduce_all(
        low, high, core, 1.0 / nlat_all, mixed, lambda x: x.reshape(channels, lat_dev, lon_dev)
    )
    return field_grad, weight_grad


def solution(mesh):
    fine = Mesh(mesh.devices.reshape(4, 2, 2, 8, 2), ("y", "x_lo", "core", "z", "x_hi"))
    split = P(None, LAT, LON)
    return jax.shard_map(
        local,
        mesh=fine,
        in_specs=(split, split, P(), P(), P()),
        out_specs=(split, P()),
        check_vma=False,
    )
```

```python
import functools

import jax
import jax.numpy as jnp
from jax import lax
from jax.experimental import pallas as pl
from jax.experimental.pallas import tpu as pltpu
from jax.sharding import Mesh, PartitionSpec as P

LAT = ("y", "x_lo", "core")
LON = ("z", "x_hi")
PLANE = ("y", "x_hi", "x_lo")
BLOCK = 32
bf16, f32 = jnp.bfloat16, jnp.float32


def pairs(axes, near, closed):
    count = 1
    for axis in axes:
        count *= lax.axis_size(axis)
    if near:
        return [(i, i ^ 1) for i in range(count)]
    far = [(i, (i + 1 - 2 * (i % 2 == 0)) % count) for i in range(count)]
    return far if closed else far[1:-1]


def parity(axes):
    return lax.rem(lax.axis_index(axes[-1]), 2)


def held_rows(lat_dev, half, nlat_all):
    above = lax.axis_index(LAT) * lat_dev - half
    held = min(16, nlat_all)
    return above, jnp.clip(above, 0, nlat_all - held), held


def tap_rows(basis_table, lon_reach, start, near):
    tap_count = basis_table.shape[3]
    table = lax.dynamic_slice_in_dim(basis_table, start, near, 1)
    reach = lax.dynamic_slice_in_dim(lon_reach, start, near, 0)
    offset = jnp.abs(lax.iota(jnp.int32, tap_count) - tap_count // 2)
    table = jnp.where((offset[None, :] <= reach[:, None])[None, :, None, :], table, jnp.zeros_like(table))
    return jnp.transpose(table, (0, 2, 1, 3))


def rim_kernel(main, near, far, second, first):
    lat_dev, lon_dev, _ = main.shape
    half, side = near.shape[0], first.shape[1]
    odd_lon, odd_lat = parity(LON), parity(LAT)
    for even in (0, 1):
        last = lon_dev - side

        @pl.when(odd_lon != even)
        def _():
            for ref, at in ((first, last if even else 0), (second, 0 if even else last)):
                ref[half : half + lat_dev] = main[:, at : at + side, :]
                own = slice(at, at + side)
                outer = slice(side, 2 * side) if at else slice(0, side)
                for upper in (0, 1):

                    @pl.when(odd_lat != upper)
                    def _():
                        above, below = slice(0, half), slice(half + lat_dev, None)
                        ref[above if upper else below] = far[:, outer, :]
                        ref[below if upper else above] = near[:, own, :]


def convolve(band, ext, place, q_ref):
    basis_count, lat_dev, columns, _ = q_ref.shape
    row_span = ext.shape[0] - lat_dev + 1
    for i in range(lat_dev):
        for j in range(columns // BLOCK):
            parts = [ext[(i + row_span - 1 - s,) + place(j)] for s in range(row_span)]
            window = jnp.concatenate(parts + [jnp.zeros_like(parts[0])], axis=0)
            out = jnp.dot(band[i], window, preferred_element_type=f32).astype(bf16)
            for k in range(basis_count):
                q_ref[k, i, j * BLOCK : (j + 1) * BLOCK, :] = out[k * BLOCK : (k + 1) * BLOCK, :]


def build_band(off, taps, band, lines):
    basis_count, row_span, near, tap_count = taps.shape
    lat_dev = band.shape[0]
    wide = 2 * BLOCK
    tap = lax.broadcasted_iota(jnp.int32, (tap_count, 128), 0)
    lane = lax.broadcasted_iota(jnp.int32, (tap_count, 128), 1)
    lines[...] = jnp.zeros_like(lines)
    for s in range(row_span):
        turn = (lane == s % 2 * wide + tap_count - 1 - tap).astype(bf16)
        for k in range(basis_count):
            lines[k, s, 8 : 8 + near, :] = jnp.dot(taps[k, s], turn, preferred_element_type=f32)
    base = off + 8 + row_span - 1
    for k in range(basis_count):
        for p in range((row_span + 1) // 2):
            pair = lines[k, 2 * p, pl.ds(base - 2 * p, lat_dev), :]
            if 2 * p + 1 < row_span:
                pair = pair + lines[k, 2 * p + 1, pl.ds(base - 2 * p - 1, lat_dev), :]
            for i in range(lat_dev):
                line = jnp.broadcast_to(pair[i : i + 1, :], (BLOCK, 128))
                line = pltpu.roll(line, 0, 1, stride=1, stride_axis=0)
                band[i, k * BLOCK : (k + 1) * BLOCK, p * 128 : (p + 1) * 128] = line.astype(bf16)


def cut_fields(f_ref, f_mid, f_edge):
    wide = 2 * BLOCK
    lane = lax.broadcasted_iota(jnp.int32, (1, 128), 1)
    for i in range(0, f_ref.shape[1] // 128, 2):
        even = f_ref[:, i * 128 : (i + 1) * 128].astype(f32)
        odd = f_ref[:, (i + 1) * 128 : (i + 2) * 128].astype(f32)
        back = lambda x: pltpu.roll(x, 128 - BLOCK, 1)
        ahead = lambda x: pltpu.roll(x, BLOCK, 1)
        at = slice(i * wide, (i + 2) * wide)
        f_mid[:, at] = jnp.where(lane < wide, back(even), ahead(odd)).astype(bf16)
        f_edge[:, at] = jnp.where(lane < wide, ahead(even), back(odd)).astype(bf16)


def middle_kernel(nlat_all, taps, f_ref, main, near, far, rest, band, f_edge, q_ref, total, window, lines, f_mid, ext):
    lat_dev, lon_dev, channels = main.shape
    half, side = near.shape[0], BLOCK // 2
    inner = window.shape[2]
    above, start, _ = held_rows(lat_dev, half, nlat_all)
    build_band(above - start, taps, band, lines)
    cut_fields(f_ref, f_mid, f_edge)
    ext[half : half + lat_dev] = main[...]
    odd_lat = parity(LAT)
    for upper in (0, 1):

        @pl.when(odd_lat != upper)
        def _():
            above, below = slice(0, half), slice(half + lat_dev, None)
            ext[below if upper else above] = near[...]
            other = above if upper else below
            ext[other, :side, :] = far[:, :side, :]
            ext[other, side : lon_dev - side, :] = rest[...]
            ext[other, lon_dev - side :, :] = far[:, side:, :]

    window[:, 0] = ext[:, lon_dev - inner :, :]
    window[:, 1] = ext[:, :inner, :]
    convolve(band, ext, lambda j: (slice(side + j * BLOCK, side + (j + 2) * BLOCK),), q_ref)
    for k in range(q_ref.shape[0]):
        cells = q_ref[k].reshape(f_mid.shape[1], channels)
        total[k] = jnp.dot(f_mid[...], cells, preferred_element_type=f32)


def edge_kernel(band, window, far, near, f_ref, total, w_ref, q_ref, low, high, w_out, ext, sem):
    fetch = pltpu.make_async_copy(w_ref, w_out, sem)
    fetch.start()
    channels = window.shape[3]
    side, inner = near.shape[1], window.shape[2]
    ext[:, 0, :inner, :] = window[:, 0]
    ext[:, 1, side:, :] = window[:, 1]
    odd_lon = parity(LON)
    for even in (0, 1):

        @pl.when(odd_lon != even)
        def _():
            ext[:, 0, inner:, :] = (near if even else far)[...]
            ext[:, 1, :side, :] = (far if even else near)[...]

    convolve(band, ext, lambda j: (j,), q_ref)
    for k in range(q_ref.shape[0]):
        cells = q_ref[k].reshape(f_ref.shape[1], channels)
        out = total[k] + jnp.dot(f_ref[...], cells, preferred_element_type=f32)
        low[k] = out[:, : channels // 2]
        high[k] = out[:, channels // 2 :]
    fetch.wait()


def call(kernel, out_shape, operands, scratch=(), hbm=0, flops=10**9, mib=16):
    vmem = pl.BlockSpec(memory_space=pltpu.VMEM)
    return pl.pallas_call(
        kernel,
        out_shape=out_shape,
        in_specs=[vmem] * (len(operands) - hbm) + [pl.BlockSpec(memory_space=pl.ANY)] * hbm,
        out_specs=jax.tree.map(lambda _: vmem, out_shape),
        scratch_shapes=list(scratch),
        compiler_params=pltpu.CompilerParams(vmem_limit_bytes=mib * 1024 * 1024),
        cost_estimate=pl.CostEstimate(flops=flops, bytes_accessed=10**6, transcendentals=0),
    )(*operands)


def mix_kernel(w_ref, mid_ref, edge_ref, out_ref):
    basis_count, lat_dev, columns, channels = mid_ref.shape
    for i in range(0, lat_dev, 2):
        total = jnp.zeros((channels, 4 * columns), f32)
        for k in range(basis_count):
            parts = []
            for row in (i, i + 1):
                parts += [edge_ref[k, row, BLOCK:], mid_ref[k, row], edge_ref[k, row, :BLOCK]]
            total += lax.dot_general(
                w_ref[k], jnp.concatenate(parts, axis=0), (((1,), (1,)), ((), ())), preferred_element_type=f32
            )
        out_ref[:, i * 2 * columns : (i + 2) * 2 * columns] = total.astype(bf16)


def place_kernel(own, half_ref, *refs):
    out, wide, sems = refs[-3:]
    basis_count, _, columns = half_ref.shape
    at = lax.axis_index("core") if own else 1 - lax.axis_index("core")
    at = pl.ds(pl.multiple_of(at * columns, columns), columns)
    parts = sems.shape[0]
    size = basis_count // parts
    copies = []
    for part in range(parts):
        rows = slice(part * size, (part + 1) * size)
        wide[rows] = half_ref[rows].astype(f32)
        copies.append(pltpu.make_async_copy(wide.at[rows], out.at[rows, :, at], sems.at[part]))
        copies[-1].start()
    for copy in copies:
        copy.wait()


def place(half, own, into=None):
    basis_count, channels, columns = half.shape
    hbm = pl.BlockSpec(memory_space=pl.ANY)
    operands = (half,) if into is None else (half, into)
    return pl.pallas_call(
        functools.partial(place_kernel, own),
        out_shape=jax.ShapeDtypeStruct((basis_count, channels, 2 * columns), f32),
        in_specs=[pl.BlockSpec(memory_space=pltpu.VMEM)] + [hbm] * (len(operands) - 1),
        out_specs=hbm,
        scratch_shapes=[pltpu.VMEM(half.shape, f32), pltpu.SemaphoreType.DMA((3,))],
        input_output_aliases={} if into is None else {1: 0},
        compiler_params=pltpu.CompilerParams(vmem_limit_bytes=4 * 1024 * 1024),
        cost_estimate=pl.CostEstimate(flops=10**6, bytes_accessed=10**6, transcendentals=0),
    )(*operands)


def all_to_all(x, axes):
    return lax.all_to_all(x, axes, 0, 0, tiled=True)


def to_all(x, count):
    return jnp.broadcast_to(x[None], (count,) + x.shape)


def reduce_all(low, high, core, scale, beside):
    swap = [(0, 1), (1, 0)]
    basis_count, channels, half = low.shape
    plane = 1
    for axis in PLANE:
        plane *= lax.axis_size(axis)
    depth = lax.axis_size("z")
    keep, send = jnp.where(core == 0, low, high), jnp.where(core == 0, high, low)
    came, beside = lax.optimization_barrier((lax.ppermute(send, "core", swap), beside))
    own = keep + came
    own = own.reshape(plane, -1, half).astype(bf16)
    own = jnp.sum(all_to_all(own, PLANE).astype(f32), axis=0).astype(bf16)
    own = jnp.sum(all_to_all(to_all(own, depth), ("z",)).astype(f32), axis=0)
    own = (own * scale).astype(bf16)
    own = all_to_all(to_all(own, plane), PLANE).reshape(basis_count, channels, half)
    other, summed = lax.optimization_barrier((lax.ppermute(own, "core", swap), place(own, True)))
    return place(other, False, summed), beside


def local(fields, grad_out, weight, basis_table, lon_reach):
    channels, lat_dev, lon_dev = fields.shape
    basis_count, nlat_all, row_span, tap_count = basis_table.shape
    half, side = row_span // 2, tap_count // 2
    near, wide = lat_dev + 2 * half, 2 * BLOCK
    shape = jax.ShapeDtypeStruct
    core = lax.axis_index("core")
    _, start, held = held_rows(lat_dev, half, nlat_all)
    upper = core == 0
    main = jnp.transpose(grad_out, (1, 2, 0))
    last, first = main[lat_dev - half :], main[:half]
    to_near, to_far = jnp.where(upper, last, first), jnp.where(upper, first, last)
    outer = jnp.concatenate([to_far[:, :side], to_far[:, lon_dev - side :]], axis=1)
    far_lat = lax.ppermute(outer, LAT, pairs(LAT, False, False))
    near_lat = lax.ppermute(to_near, LAT, pairs(LAT, True, False))
    rest_lat = lax.ppermute(to_far[:, side : lon_dev - side], LAT, pairs(LAT, False, False))
    rim = shape((near, side, channels), bf16)
    to_far, to_near = call(rim_kernel, (rim, rim), (main, near_lat, far_lat), flops=10**6, mib=4)
    far_lon = lax.ppermute(to_far, LON, pairs(LON, False, True))
    near_lon = lax.ppermute(to_near, LON, pairs(LON, True, True))
    taps = tap_rows(basis_table, lon_reach, start, held)
    q_shape = shape((basis_count, lat_dev, wide, channels), bf16)
    columns = shape((channels, lat_dev * wide), bf16)
    part = shape((basis_count, channels, channels // 2), f32)
    band, f_edge, q_mid, total, window = call(
        functools.partial(middle_kernel, nlat_all),
        (
            shape((lat_dev, basis_count * BLOCK, (row_span + 1) * wide), bf16),
            columns,
            q_shape,
            shape((basis_count, channels, channels), f32),
            shape((near, 2, wide - side, channels), bf16),
        ),
        (taps, fields.reshape(channels, lat_dev * lon_dev), main, near_lat, far_lat, rest_lat),
        [
            pltpu.VMEM((basis_count, row_span, held + 16, 128), f32),
            pltpu.VMEM(columns.shape, bf16),
            pltpu.VMEM((near, lon_dev, channels), bf16),
        ],
    )
    q_edge, low, high, weight = call(
        edge_kernel,
        (q_shape, part, part, shape(weight.shape, bf16)),
        (band, window, far_lon, near_lon, f_edge, total, weight),
        [pltpu.VMEM((near, 2, wide, channels), bf16), pltpu.SemaphoreType.DMA],
        hbm=1,
    )
    mixed = call(mix_kernel, shape((channels, lat_dev * lon_dev), bf16), (weight, q_mid, q_edge))
    field_grad = mixed.reshape(channels, lat_dev, lon_dev)
    weight_grad, field_grad = reduce_all(low, high, core, 1.0 / nlat_all, field_grad)
    return field_grad, weight_grad


def solution(mesh):
    fine = Mesh(mesh.devices.reshape(4, 2, 2, 8, 2), ("y", "x_lo", "core", "z", "x_hi"))
    split = P(None, LAT, LON)
    return jax.shard_map(
        local,
        mesh=fine,
        in_specs=(split, split, P(), P(), P()),
        out_specs=(split, P()),
        check_vma=False,
    )
```

```python
import functools

import jax
import jax.numpy as jnp
from jax import lax
from jax.experimental import pallas as pl
from jax.experimental.pallas import tpu as pltpu
from jax.sharding import Mesh, PartitionSpec as P

LAT = ("y", "x_lo", "core")
LON = ("z", "x_hi")
PLANE = ("y", "x_hi", "x_lo")
BLOCK = 32
bf16, f32 = jnp.bfloat16, jnp.float32


def pairs(axes, near, closed):
    count = 1
    for axis in axes:
        count *= lax.axis_size(axis)
    if near:
        return [(i, i ^ 1) for i in range(count)]
    far = [(i, (i + 1 - 2 * (i % 2 == 0)) % count) for i in range(count)]
    return far if closed else far[1:-1]


def parity(axes):
    return lax.rem(lax.axis_index(axes[-1]), 2)


def held_rows(lat_dev, half, nlat_all):
    above = lax.axis_index(LAT) * lat_dev - half
    held = min(16, nlat_all)
    return above, jnp.clip(above, 0, nlat_all - held), held


def tap_rows(basis_table, lon_reach, start, near):
    tap_count = basis_table.shape[3]
    table = lax.dynamic_slice_in_dim(basis_table, start, near, 1)
    reach = lax.dynamic_slice_in_dim(lon_reach, start, near, 0)
    offset = jnp.abs(lax.iota(jnp.int32, tap_count) - tap_count // 2)
    table = jnp.where((offset[None, :] <= reach[:, None])[None, :, None, :], table, jnp.zeros_like(table))
    return jnp.transpose(table, (0, 2, 1, 3))


def rim_kernel(main, near, far, second, first):
    lat_dev, lon_dev, _ = main.shape
    half, side = near.shape[0], first.shape[1]
    odd_lon, odd_lat = parity(LON), parity(LAT)
    for even in (0, 1):
        last = lon_dev - side

        @pl.when(odd_lon != even)
        def _():
            for ref, at in ((first, last if even else 0), (second, 0 if even else last)):
                ref[half : half + lat_dev] = main[:, at : at + side, :]
                own = slice(at, at + side)
                outer = slice(side, 2 * side) if at else slice(0, side)
                for upper in (0, 1):

                    @pl.when(odd_lat != upper)
                    def _():
                        above, below = slice(0, half), slice(half + lat_dev, None)
                        ref[above if upper else below] = far[:, outer, :]
                        ref[below if upper else above] = near[:, own, :]


def convolve(band, ext, place, q_ref):
    basis_count, lat_dev, columns, _ = q_ref.shape
    row_span = ext.shape[0] - lat_dev + 1
    for i in range(lat_dev):
        for j in range(columns // BLOCK):
            parts = [ext[(i + row_span - 1 - s,) + place(j)] for s in range(row_span)]
            window = jnp.concatenate(parts + [jnp.zeros_like(parts[0])], axis=0)
            out = jnp.dot(band[i], window, preferred_element_type=f32).astype(bf16)
            for k in range(basis_count):
                q_ref[k, i, j * BLOCK : (j + 1) * BLOCK, :] = out[k * BLOCK : (k + 1) * BLOCK, :]


def build_band(off, taps, band, lines):
    basis_count, row_span, near, tap_count = taps.shape
    lat_dev = band.shape[0]
    wide = 2 * BLOCK
    tap = lax.broadcasted_iota(jnp.int32, (tap_count, 128), 0)
    lane = lax.broadcasted_iota(jnp.int32, (tap_count, 128), 1)
    lines[...] = jnp.zeros_like(lines)
    for s in range(row_span):
        turn = (lane == s % 2 * wide + tap_count - 1 - tap).astype(bf16)
        for k in range(basis_count):
            lines[k, s, 8 : 8 + near, :] = jnp.dot(taps[k, s], turn, preferred_element_type=f32)
    base = off + 8 + row_span - 1
    for k in range(basis_count):
        for p in range((row_span + 1) // 2):
            pair = lines[k, 2 * p, pl.ds(base - 2 * p, lat_dev), :]
            if 2 * p + 1 < row_span:
                pair = pair + lines[k, 2 * p + 1, pl.ds(base - 2 * p - 1, lat_dev), :]
            for i in range(lat_dev):
                line = jnp.broadcast_to(pair[i : i + 1, :], (BLOCK, 128))
                line = pltpu.roll(line, 0, 1, stride=1, stride_axis=0)
                band[i, k * BLOCK : (k + 1) * BLOCK, p * 128 : (p + 1) * 128] = line.astype(bf16)


def cut_fields(f_ref, f_mid, f_edge):
    wide = 2 * BLOCK
    lane = lax.broadcasted_iota(jnp.int32, (1, 128), 1)
    for i in range(0, f_ref.shape[1] // 128, 2):
        even = f_ref[:, i * 128 : (i + 1) * 128].astype(f32)
        odd = f_ref[:, (i + 1) * 128 : (i + 2) * 128].astype(f32)
        back = lambda x: pltpu.roll(x, 128 - BLOCK, 1)
        ahead = lambda x: pltpu.roll(x, BLOCK, 1)
        at = slice(i * wide, (i + 2) * wide)
        f_mid[:, at] = jnp.where(lane < wide, back(even), ahead(odd)).astype(bf16)
        f_edge[:, at] = jnp.where(lane < wide, ahead(even), back(odd)).astype(bf16)


def middle_kernel(nlat_all, taps, f_ref, main, near, far, rest, band, f_edge, q_ref, total, window, lines, f_mid, ext):
    lat_dev, lon_dev, channels = main.shape
    half, side = near.shape[0], BLOCK // 2
    inner = window.shape[2]
    above, start, _ = held_rows(lat_dev, half, nlat_all)
    build_band(above - start, taps, band, lines)
    cut_fields(f_ref, f_mid, f_edge)
    ext[half : half + lat_dev] = main[...]
    odd_lat = parity(LAT)
    for upper in (0, 1):

        @pl.when(odd_lat != upper)
        def _():
            above, below = slice(0, half), slice(half + lat_dev, None)
            ext[below if upper else above] = near[...]
            other = above if upper else below
            ext[other, :side, :] = far[:, :side, :]
            ext[other, side : lon_dev - side, :] = rest[...]
            ext[other, lon_dev - side :, :] = far[:, side:, :]

    window[:, 0] = ext[:, lon_dev - inner :, :]
    window[:, 1] = ext[:, :inner, :]
    convolve(band, ext, lambda j: (slice(side + j * BLOCK, side + (j + 2) * BLOCK),), q_ref)
    for k in range(q_ref.shape[0]):
        cells = q_ref[k].reshape(f_mid.shape[1], channels)
        total[k] = jnp.dot(f_mid[...], cells, preferred_element_type=f32)


def edge_kernel(band, window, far, near, f_ref, total, w_ref, q_ref, low, high, w_out, ext, sem):
    fetch = pltpu.make_async_copy(w_ref, w_out, sem)
    fetch.start()
    channels = window.shape[3]
    side, inner = near.shape[1], window.shape[2]
    ext[:, 0, :inner, :] = window[:, 0]
    ext[:, 1, side:, :] = window[:, 1]
    odd_lon = parity(LON)
    for even in (0, 1):

        @pl.when(odd_lon != even)
        def _():
            ext[:, 0, inner:, :] = (near if even else far)[...]
            ext[:, 1, :side, :] = (far if even else near)[...]

    convolve(band, ext, lambda j: (j,), q_ref)
    for k in range(q_ref.shape[0]):
        cells = q_ref[k].reshape(f_ref.shape[1], channels)
        out = total[k] + jnp.dot(f_ref[...], cells, preferred_element_type=f32)
        low[k] = out[:, : channels // 2]
        high[k] = out[:, channels // 2 :]
    fetch.wait()


def call(kernel, out_shape, operands, scratch=(), hbm=0, flops=10**9, mib=16):
    vmem = pl.BlockSpec(memory_space=pltpu.VMEM)
    return pl.pallas_call(
        kernel,
        out_shape=out_shape,
        in_specs=[vmem] * (len(operands) - hbm) + [pl.BlockSpec(memory_space=pl.ANY)] * hbm,
        out_specs=jax.tree.map(lambda _: vmem, out_shape),
        scratch_shapes=list(scratch),
        compiler_params=pltpu.CompilerParams(vmem_limit_bytes=mib * 1024 * 1024),
        cost_estimate=pl.CostEstimate(flops=flops, bytes_accessed=10**6, transcendentals=0),
    )(*operands)


def mix_kernel(w_ref, mid_ref, edge_ref, out_ref):
    basis_count, lat_dev, columns, channels = mid_ref.shape
    for i in range(0, lat_dev, 2):
        total = jnp.zeros((channels, 4 * columns), f32)
        for k in range(basis_count):
            parts = []
            for row in (i, i + 1):
                parts += [edge_ref[k, row, BLOCK:], mid_ref[k, row], edge_ref[k, row, :BLOCK]]
            total += lax.dot_general(
                w_ref[k], jnp.concatenate(parts, axis=0), (((1,), (1,)), ((), ())), preferred_element_type=f32
            )
        out_ref[:, i * 2 * columns : (i + 2) * 2 * columns] = total.astype(bf16)


def place_kernel(own, half_ref, *refs):
    out, wide, sems = refs[-3:]
    basis_count, _, columns = half_ref.shape
    at = lax.axis_index("core") if own else 1 - lax.axis_index("core")
    at = pl.ds(pl.multiple_of(at * columns, columns), columns)
    parts = sems.shape[0]
    size = basis_count // parts
    copies = []
    for part in range(parts):
        rows = slice(part * size, (part + 1) * size)
        wide[rows] = half_ref[rows].astype(f32)
        copies.append(pltpu.make_async_copy(wide.at[rows], out.at[rows, :, at], sems.at[part]))
        copies[-1].start()
    for copy in copies:
        copy.wait()


def place(half, own, into=None):
    basis_count, channels, columns = half.shape
    hbm = pl.BlockSpec(memory_space=pl.ANY)
    operands = (half,) if into is None else (half, into)
    return pl.pallas_call(
        functools.partial(place_kernel, own),
        out_shape=jax.ShapeDtypeStruct((basis_count, channels, 2 * columns), f32),
        in_specs=[pl.BlockSpec(memory_space=pltpu.VMEM)] + [hbm] * (len(operands) - 1),
        out_specs=hbm,
        scratch_shapes=[pltpu.VMEM(half.shape, f32), pltpu.SemaphoreType.DMA((3,))],
        input_output_aliases={} if into is None else {1: 0},
        compiler_params=pltpu.CompilerParams(vmem_limit_bytes=4 * 1024 * 1024),
        cost_estimate=pl.CostEstimate(flops=10**6, bytes_accessed=10**6, transcendentals=0),
    )(*operands)


def all_to_all(x, axes):
    return lax.all_to_all(x, axes, 0, 0, tiled=True)


def to_all(x, count):
    return jnp.broadcast_to(x[None], (count,) + x.shape)


def reduce_all(low, high, core, scale, beside, finish):
    swap = [(0, 1), (1, 0)]
    basis_count, channels, half = low.shape
    plane = 1
    for axis in PLANE:
        plane *= lax.axis_size(axis)
    depth = lax.axis_size("z")
    keep, send = jnp.where(core == 0, low, high), jnp.where(core == 0, high, low).astype(bf16)
    came, beside = lax.optimization_barrier((lax.ppermute(send, "core", swap), beside))
    own = keep + came.astype(f32)
    own = own.reshape(plane, -1, half).astype(bf16)
    own = jnp.sum(all_to_all(own, PLANE).astype(f32), axis=0).astype(bf16)
    own = jnp.sum(all_to_all(to_all(own, depth), ("z",)).astype(f32), axis=0)
    own = (own * scale).astype(bf16)
    own = all_to_all(to_all(own, plane), PLANE).reshape(basis_count, channels, half)
    beside = finish(beside)
    other, summed, beside = lax.optimization_barrier((lax.ppermute(own, "core", swap), place(own, True), beside))
    return place(other, False, summed), beside


def local(fields, grad_out, weight, basis_table, lon_reach):
    channels, lat_dev, lon_dev = fields.shape
    basis_count, nlat_all, row_span, tap_count = basis_table.shape
    half, side = row_span // 2, tap_count // 2
    near, wide = lat_dev + 2 * half, 2 * BLOCK
    shape = jax.ShapeDtypeStruct
    core = lax.axis_index("core")
    _, start, held = held_rows(lat_dev, half, nlat_all)
    upper = core == 0
    main = jnp.transpose(grad_out, (1, 2, 0))
    last, first = main[lat_dev - half :], main[:half]
    to_near, to_far = jnp.where(upper, last, first), jnp.where(upper, first, last)
    outer = jnp.concatenate([to_far[:, :side], to_far[:, lon_dev - side :]], axis=1)
    far_lat = lax.ppermute(outer, LAT, pairs(LAT, False, False))
    near_lat = lax.ppermute(to_near, LAT, pairs(LAT, True, False))
    rest, near_lat = lax.optimization_barrier((to_far[:, side : lon_dev - side], near_lat))
    rest_lat = lax.ppermute(rest, LAT, pairs(LAT, False, False))
    rim = shape((near, side, channels), bf16)
    to_far, to_near = call(rim_kernel, (rim, rim), (main, near_lat, far_lat), flops=10**6, mib=4)
    far_lon = lax.ppermute(to_far, LON, pairs(LON, False, True))
    near_lon = lax.ppermute(to_near, LON, pairs(LON, True, True))
    taps = tap_rows(basis_table, lon_reach, start, held)
    q_shape = shape((basis_count, lat_dev, wide, channels), bf16)
    columns = shape((channels, lat_dev * wide), bf16)
    part = shape((basis_count, channels, channels // 2), f32)
    band, f_edge, q_mid, total, window = call(
        functools.partial(middle_kernel, nlat_all),
        (
            shape((lat_dev, basis_count * BLOCK, (row_span + 1) * wide), bf16),
            columns,
            q_shape,
            shape((basis_count, channels, channels), f32),
            shape((near, 2, wide - side, channels), bf16),
        ),
        (taps, fields.reshape(channels, lat_dev * lon_dev), main, near_lat, far_lat, rest_lat),
        [
            pltpu.VMEM((basis_count, row_span, held + 16, 128), f32),
            pltpu.VMEM(columns.shape, bf16),
            pltpu.VMEM((near, lon_dev, channels), bf16),
        ],
    )
    q_edge, low, high, weight = call(
        edge_kernel,
        (q_shape, part, part, shape(weight.shape, bf16)),
        (band, window, far_lon, near_lon, f_edge, total, weight),
        [pltpu.VMEM((near, 2, wide, channels), bf16), pltpu.SemaphoreType.DMA],
        hbm=1,
    )
    mixed = call(mix_kernel, shape((channels, lat_dev * lon_dev), bf16), (weight, q_mid, q_edge))
    weight_grad, field_grad = reduce_all(
        low, high, core, 1.0 / nlat_all, mixed, lambda x: x.reshape(channels, lat_dev, lon_dev)
    )
    return field_grad, weight_grad


def solution(mesh):
    fine = Mesh(mesh.devices.reshape(4, 2, 2, 8, 2), ("y", "x_lo", "core", "z", "x_hi"))
    split = P(None, LAT, LON)
    return jax.shard_map(
        local,
        mesh=fine,
        in_specs=(split, split, P(), P(), P()),
        out_specs=(split, P()),
        check_vma=False,
    )
```

```python
import functools

import jax
import jax.numpy as jnp
from jax import lax
from jax.experimental import pallas as pl
from jax.experimental.pallas import tpu as pltpu
from jax.sharding import Mesh, PartitionSpec as P

LAT = ("y", "x_lo", "core")
LON = ("z", "x_hi")
PLANE = ("y", "x_hi", "x_lo")
BLOCK = 32
bf16, f32 = jnp.bfloat16, jnp.float32


def pairs(axes, near, closed):
    count = 1
    for axis in axes:
        count *= lax.axis_size(axis)
    if near:
        return [(i, i ^ 1) for i in range(count)]
    far = [(i, (i + 1 - 2 * (i % 2 == 0)) % count) for i in range(count)]
    return far if closed else far[1:-1]


def parity(axes):
    return lax.rem(lax.axis_index(axes[-1]), 2)


def held_rows(lat_dev, half, nlat_all):
    above = lax.axis_index(LAT) * lat_dev - half
    held = min(16, nlat_all)
    return above, jnp.clip(above, 0, nlat_all - held), held


def tap_rows(basis_table, lon_reach, start, near):
    tap_count = basis_table.shape[3]
    table = lax.dynamic_slice_in_dim(basis_table, start, near, 1)
    reach = lax.dynamic_slice_in_dim(lon_reach, start, near, 0)
    offset = jnp.abs(lax.iota(jnp.int32, tap_count) - tap_count // 2)
    table = jnp.where((offset[None, :] <= reach[:, None])[None, :, None, :], table, jnp.zeros_like(table))
    return jnp.transpose(table, (0, 2, 1, 3))


def rim_kernel(main, near, far, second, first):
    lat_dev, lon_dev, _ = main.shape
    half, side = near.shape[0], first.shape[1]
    odd_lon, odd_lat = parity(LON), parity(LAT)
    for even in (0, 1):
        last = lon_dev - side

        @pl.when(odd_lon != even)
        def _():
            for ref, at in ((first, last if even else 0), (second, 0 if even else last)):
                ref[half : half + lat_dev] = main[:, at : at + side, :]
                own = slice(at, at + side)
                outer = slice(side, 2 * side) if at else slice(0, side)
                for upper in (0, 1):

                    @pl.when(odd_lat != upper)
                    def _():
                        above, below = slice(0, half), slice(half + lat_dev, None)
                        ref[above if upper else below] = far[:, outer, :]
                        ref[below if upper else above] = near[:, own, :]


def convolve(band, ext, place, q_ref):
    basis_count, lat_dev, columns, _ = q_ref.shape
    row_span = ext.shape[0] - lat_dev + 1
    for i in range(lat_dev):
        for j in range(columns // BLOCK):
            parts = [ext[(i + row_span - 1 - s,) + place(j)] for s in range(row_span)]
            window = jnp.concatenate(parts + [jnp.zeros_like(parts[0])], axis=0)
            out = jnp.dot(band[i], window, preferred_element_type=f32).astype(bf16)
            for k in range(basis_count):
                q_ref[k, i, j * BLOCK : (j + 1) * BLOCK, :] = out[k * BLOCK : (k + 1) * BLOCK, :]


def build_band(off, taps, band, lines):
    basis_count, row_span, near, tap_count = taps.shape
    lat_dev = band.shape[0]
    wide = 2 * BLOCK
    tap = lax.broadcasted_iota(jnp.int32, (tap_count, 128), 0)
    lane = lax.broadcasted_iota(jnp.int32, (tap_count, 128), 1)
    lines[...] = jnp.zeros_like(lines)
    for s in range(row_span):
        turn = (lane == s % 2 * wide + tap_count - 1 - tap).astype(bf16)
        for k in range(basis_count):
            lines[k, s, 8 : 8 + near, :] = jnp.dot(taps[k, s], turn, preferred_element_type=f32)
    base = off + 8 + row_span - 1
    for k in range(basis_count):
        for p in range((row_span + 1) // 2):
            pair = lines[k, 2 * p, pl.ds(base - 2 * p, lat_dev), :]
            if 2 * p + 1 < row_span:
                pair = pair + lines[k, 2 * p + 1, pl.ds(base - 2 * p - 1, lat_dev), :]
            for i in range(lat_dev):
                line = jnp.broadcast_to(pair[i : i + 1, :], (BLOCK, 128))
                line = pltpu.roll(line, 0, 1, stride=1, stride_axis=0)
                band[i, k * BLOCK : (k + 1) * BLOCK, p * 128 : (p + 1) * 128] = line.astype(bf16)


def cut_fields(f_ref, f_mid, f_edge):
    wide = 2 * BLOCK
    lane = lax.broadcasted_iota(jnp.int32, (1, 128), 1)
    for i in range(0, f_ref.shape[1] // 128, 2):
        even = f_ref[:, i * 128 : (i + 1) * 128].astype(f32)
        odd = f_ref[:, (i + 1) * 128 : (i + 2) * 128].astype(f32)
        back = lambda x: pltpu.roll(x, 128 - BLOCK, 1)
        ahead = lambda x: pltpu.roll(x, BLOCK, 1)
        at = slice(i * wide, (i + 2) * wide)
        f_mid[:, at] = jnp.where(lane < wide, back(even), ahead(odd)).astype(bf16)
        f_edge[:, at] = jnp.where(lane < wide, ahead(even), back(odd)).astype(bf16)


def middle_kernel(nlat_all, taps, f_ref, main, near, far, rest, band, f_edge, q_ref, total, window, lines, f_mid, ext):
    lat_dev, lon_dev, channels = main.shape
    half, side = near.shape[0], BLOCK // 2
    inner = window.shape[2]
    above, start, _ = held_rows(lat_dev, half, nlat_all)
    build_band(above - start, taps, band, lines)
    cut_fields(f_ref, f_mid, f_edge)
    ext[half : half + lat_dev] = main[...]
    odd_lat = parity(LAT)
    for upper in (0, 1):

        @pl.when(odd_lat != upper)
        def _():
            above, below = slice(0, half), slice(half + lat_dev, None)
            ext[below if upper else above] = near[...]
            other = above if upper else below
            ext[other, :side, :] = far[:, :side, :]
            ext[other, side : lon_dev - side, :] = rest[...]
            ext[other, lon_dev - side :, :] = far[:, side:, :]

    window[:, 0] = ext[:, lon_dev - inner :, :]
    window[:, 1] = ext[:, :inner, :]
    convolve(band, ext, lambda j: (slice(side + j * BLOCK, side + (j + 2) * BLOCK),), q_ref)
    for k in range(q_ref.shape[0]):
        cells = q_ref[k].reshape(f_mid.shape[1], channels)
        total[k] = jnp.dot(f_mid[...], cells, preferred_element_type=f32)


def edge_kernel(band, window, far, near, f_ref, total, w_ref, q_ref, low, high, w_out, ext, sem):
    fetch = pltpu.make_async_copy(w_ref, w_out, sem)
    fetch.start()
    channels = window.shape[3]
    side, inner = near.shape[1], window.shape[2]
    ext[:, 0, :inner, :] = window[:, 0]
    ext[:, 1, side:, :] = window[:, 1]
    odd_lon = parity(LON)
    for even in (0, 1):

        @pl.when(odd_lon != even)
        def _():
            ext[:, 0, inner:, :] = (near if even else far)[...]
            ext[:, 1, :side, :] = (far if even else near)[...]

    convolve(band, ext, lambda j: (j,), q_ref)
    for k in range(q_ref.shape[0]):
        cells = q_ref[k].reshape(f_ref.shape[1], channels)
        out = total[k] + jnp.dot(f_ref[...], cells, preferred_element_type=f32)
        low[k] = out[:, : channels // 2]
        high[k] = out[:, channels // 2 :]
    fetch.wait()


def call(kernel, out_shape, operands, scratch=(), hbm=0, flops=10**9, mib=16):
    vmem = pl.BlockSpec(memory_space=pltpu.VMEM)
    return pl.pallas_call(
        kernel,
        out_shape=out_shape,
        in_specs=[vmem] * (len(operands) - hbm) + [pl.BlockSpec(memory_space=pl.ANY)] * hbm,
        out_specs=jax.tree.map(lambda _: vmem, out_shape),
        scratch_shapes=list(scratch),
        compiler_params=pltpu.CompilerParams(vmem_limit_bytes=mib * 1024 * 1024),
        cost_estimate=pl.CostEstimate(flops=flops, bytes_accessed=10**6, transcendentals=0),
    )(*operands)


def mix_kernel(w_ref, mid_ref, edge_ref, out_ref):
    basis_count, lat_dev, columns, channels = mid_ref.shape
    for i in range(0, lat_dev, 2):
        total = jnp.zeros((channels, 4 * columns), f32)
        for k in range(basis_count):
            parts = []
            for row in (i, i + 1):
                parts += [edge_ref[k, row, BLOCK:], mid_ref[k, row], edge_ref[k, row, :BLOCK]]
            total += lax.dot_general(
                w_ref[k], jnp.concatenate(parts, axis=0), (((1,), (1,)), ((), ())), preferred_element_type=f32
            )
        out_ref[:, i * 2 * columns : (i + 2) * 2 * columns] = total.astype(bf16)


def place_kernel(own, half_ref, *refs):
    out, wide, sems = refs[-3:]
    basis_count, _, columns = half_ref.shape
    at = lax.axis_index("core") if own else 1 - lax.axis_index("core")
    at = pl.ds(pl.multiple_of(at * columns, columns), columns)
    parts = sems.shape[0]
    size = basis_count // parts
    copies = []
    for part in range(parts):
        rows = slice(part * size, (part + 1) * size)
        wide[rows] = half_ref[rows].astype(f32)
        copies.append(pltpu.make_async_copy(wide.at[rows], out.at[rows, :, at], sems.at[part]))
        copies[-1].start()
    for copy in copies:
        copy.wait()


def place(half, own, into=None):
    basis_count, channels, columns = half.shape
    hbm = pl.BlockSpec(memory_space=pl.ANY)
    operands = (half,) if into is None else (half, into)
    return pl.pallas_call(
        functools.partial(place_kernel, own),
        out_shape=jax.ShapeDtypeStruct((basis_count, channels, 2 * columns), f32),
        in_specs=[pl.BlockSpec(memory_space=pltpu.VMEM)] + [hbm] * (len(operands) - 1),
        out_specs=hbm,
        scratch_shapes=[pltpu.VMEM(half.shape, f32), pltpu.SemaphoreType.DMA((3,))],
        input_output_aliases={} if into is None else {1: 0},
        compiler_params=pltpu.CompilerParams(vmem_limit_bytes=4 * 1024 * 1024),
        cost_estimate=pl.CostEstimate(flops=10**6, bytes_accessed=10**6, transcendentals=0),
    )(*operands)


def all_to_all(x, axes):
    return lax.all_to_all(x, axes, 0, 0, tiled=True)


def to_all(x, count):
    return jnp.broadcast_to(x[None], (count,) + x.shape)


def reduce_all(low, high, core, scale, beside, finish):
    swap = [(0, 1), (1, 0)]
    basis_count, channels, half = low.shape
    plane = 1
    for axis in PLANE:
        plane *= lax.axis_size(axis)
    depth = lax.axis_size("z")
    keep, send = jnp.where(core == 0, low, high), jnp.where(core == 0, high, low).astype(bf16)
    came, beside = lax.optimization_barrier((lax.ppermute(send, "core", swap), beside))
    own = keep + came.astype(f32)
    own = own.reshape(plane, -1, half).astype(bf16)
    own = jnp.sum(all_to_all(own, PLANE).astype(f32), axis=0).astype(bf16)
    own = jnp.sum(all_to_all(to_all(own, depth), ("z",)).astype(f32), axis=0)
    own = (own * scale).astype(bf16)
    own = all_to_all(to_all(own, plane), PLANE).reshape(basis_count, channels, half)
    beside = finish(beside)
    other, summed, beside = lax.optimization_barrier((lax.ppermute(own, "core", swap), place(own, True), beside))
    return place(other, False, summed), beside


def local(fields, grad_out, weight, basis_table, lon_reach):
    channels, lat_dev, lon_dev = fields.shape
    basis_count, nlat_all, row_span, tap_count = basis_table.shape
    half, side = row_span // 2, tap_count // 2
    near, wide = lat_dev + 2 * half, 2 * BLOCK
    shape = jax.ShapeDtypeStruct
    core = lax.axis_index("core")
    _, start, held = held_rows(lat_dev, half, nlat_all)
    upper = core == 0
    main = jnp.transpose(grad_out, (1, 2, 0))
    last, first = main[lat_dev - half :], main[:half]
    to_near, to_far = jnp.where(upper, last, first), jnp.where(upper, first, last)
    outer = jnp.concatenate([to_far[:, :side], to_far[:, lon_dev - side :]], axis=1)
    far_lat = lax.ppermute(outer, LAT, pairs(LAT, False, False))
    near_lat = lax.ppermute(to_near, LAT, pairs(LAT, True, False))
    rest_lat = lax.ppermute(to_far[:, side : lon_dev - side], LAT, pairs(LAT, False, False))
    rim = shape((near, side, channels), bf16)
    to_far, to_near = call(rim_kernel, (rim, rim), (main, near_lat, far_lat), flops=10**6, mib=4)
    far_lon = lax.ppermute(to_far, LON, pairs(LON, False, True))
    near_lon = lax.ppermute(to_near, LON, pairs(LON, True, True))
    taps = tap_rows(basis_table, lon_reach, start, held)
    q_shape = shape((basis_count, lat_dev, wide, channels), bf16)
    columns = shape((channels, lat_dev * wide), bf16)
    part = shape((basis_count, channels, channels // 2), f32)
    band, f_edge, q_mid, total, window = call(
        functools.partial(middle_kernel, nlat_all),
        (
            shape((lat_dev, basis_count * BLOCK, (row_span + 1) * wide), bf16),
            columns,
            q_shape,
            shape((basis_count, channels, channels), f32),
            shape((near, 2, wide - side, channels), bf16),
        ),
        (taps, fields.reshape(channels, lat_dev * lon_dev), main, near_lat, far_lat, rest_lat),
        [
            pltpu.VMEM((basis_count, row_span, held + 16, 128), f32),
            pltpu.VMEM(columns.shape, bf16),
            pltpu.VMEM((near, lon_dev, channels), bf16),
        ],
    )
    q_edge, low, high, weight = call(
        edge_kernel,
        (q_shape, part, part, shape(weight.shape, bf16)),
        (band, window, far_lon, near_lon, f_edge, total, weight),
        [pltpu.VMEM((near, 2, wide, channels), bf16), pltpu.SemaphoreType.DMA],
        hbm=1,
    )
    mixed = call(mix_kernel, shape((channels, lat_dev * lon_dev), bf16), (weight, q_mid, q_edge))
    weight_grad, field_grad = reduce_all(
        low, high, core, 1.0 / nlat_all, mixed, lambda x: x.reshape(channels, lat_dev, lon_dev)
    )
    return field_grad, weight_grad


def solution(mesh):
    fine = Mesh(mesh.devices.reshape(4, 2, 2, 8, 2), ("y", "x_lo", "core", "z", "x_hi"))
    split = P(None, LAT, LON)
    return jax.shard_map(
        local,
        mesh=fine,
        in_specs=(split, split, P(), P(), P()),
        out_specs=(split, P()),
        check_vma=False,
    )
```

```python
import functools

import jax
import jax.numpy as jnp
from jax import lax
from jax.experimental import pallas as pl
from jax.experimental.pallas import tpu as pltpu
from jax.sharding import Mesh, PartitionSpec as P

LAT = ("y", "x_lo", "core")
LON = ("z", "x_hi")
PLANE = ("y", "x_hi", "x_lo")
BLOCK = 32
bf16, f32 = jnp.bfloat16, jnp.float32


def pairs(axes, near, closed):
    count = 1
    for axis in axes:
        count *= lax.axis_size(axis)
    if near:
        return [(i, i ^ 1) for i in range(count)]
    far = [(i, (i + 1 - 2 * (i % 2 == 0)) % count) for i in range(count)]
    return far if closed else far[1:-1]


def parity(axes):
    return lax.rem(lax.axis_index(axes[-1]), 2)


def held_rows(lat_dev, half, nlat_all):
    above = lax.axis_index(LAT) * lat_dev - half
    held = min(16, nlat_all)
    return above, jnp.clip(above, 0, nlat_all - held), held


def tap_rows(basis_table, lon_reach, start, near):
    tap_count = basis_table.shape[3]
    table = lax.dynamic_slice_in_dim(basis_table, start, near, 1)
    reach = lax.dynamic_slice_in_dim(lon_reach, start, near, 0)
    offset = jnp.abs(lax.iota(jnp.int32, tap_count) - tap_count // 2)
    table = jnp.where((offset[None, :] <= reach[:, None])[None, :, None, :], table, jnp.zeros_like(table))
    return jnp.transpose(table, (0, 2, 1, 3))


def own_rows(half, lat_dev):
    return (slice(half, half + lat_dev), slice(0, half)), (slice(0, lat_dev), slice(lat_dev, None))


def rim_kernel(main, far, second, first):
    lat_dev, lon_dev, _ = main.shape
    half, side = far.shape[0], first.shape[1]
    odd_lon, odd_lat = parity(LON), parity(LAT)
    last = lon_dev - side
    for odd, (own, other) in enumerate(own_rows(half, lat_dev)):
        for even in (0, 1):

            @pl.when((odd_lon != even) & (odd_lat == odd))
            def _():
                for ref, at in ((first, last if even else 0), (second, 0 if even else last)):
                    outer = slice(side, 2 * side) if at else slice(0, side)
                    ref[own] = main[:, at : at + side, :]
                    ref[other] = far[:, outer, :]


def corner_kernel(far, near, out):
    half, side = out.shape[0], far.shape[1]
    lat_dev = far.shape[0] - half
    odd_lat = parity(LAT)
    for odd, rows in enumerate((slice(lat_dev, None), slice(0, half))):

        @pl.when(odd_lat == odd)
        def _():
            out[:, :side, :] = far[rows]
            out[:, side:, :] = near[rows]


def convolve(band, ext, place, q_ref):
    basis_count, lat_dev, columns, _ = q_ref.shape
    row_span = ext.shape[0] - lat_dev + 1
    for i in range(lat_dev):
        for j in range(columns // BLOCK):
            parts = [ext[(i + row_span - 1 - s,) + place(j)] for s in range(row_span)]
            window = jnp.concatenate(parts + [jnp.zeros_like(parts[0])], axis=0)
            out = jnp.dot(band[i], window, preferred_element_type=f32).astype(bf16)
            for k in range(basis_count):
                q_ref[k, i, j * BLOCK : (j + 1) * BLOCK, :] = out[k * BLOCK : (k + 1) * BLOCK, :]


def build_band(off, taps, band, lines):
    basis_count, row_span, near, tap_count = taps.shape
    lat_dev = band.shape[0]
    wide = 2 * BLOCK
    tap = lax.broadcasted_iota(jnp.int32, (tap_count, 128), 0)
    lane = lax.broadcasted_iota(jnp.int32, (tap_count, 128), 1)
    lines[...] = jnp.zeros_like(lines)
    for s in range(row_span):
        turn = (lane == s % 2 * wide + tap_count - 1 - tap).astype(bf16)
        for k in range(basis_count):
            lines[k, s, 8 : 8 + near, :] = jnp.dot(taps[k, s], turn, preferred_element_type=f32)
    base = off + 8 + row_span - 1
    for k in range(basis_count):
        for p in range((row_span + 1) // 2):
            pair = lines[k, 2 * p, pl.ds(base - 2 * p, lat_dev), :]
            if 2 * p + 1 < row_span:
                pair = pair + lines[k, 2 * p + 1, pl.ds(base - 2 * p - 1, lat_dev), :]
            for i in range(lat_dev):
                line = jnp.broadcast_to(pair[i : i + 1, :], (BLOCK, 128))
                line = pltpu.roll(line, 0, 1, stride=1, stride_axis=0)
                band[i, k * BLOCK : (k + 1) * BLOCK, p * 128 : (p + 1) * 128] = line.astype(bf16)


def cut_fields(f_ref, f_mid, f_edge):
    wide = 2 * BLOCK
    lane = lax.broadcasted_iota(jnp.int32, (1, 128), 1)
    for i in range(0, f_ref.shape[1] // 128, 2):
        even = f_ref[:, i * 128 : (i + 1) * 128].astype(f32)
        odd = f_ref[:, (i + 1) * 128 : (i + 2) * 128].astype(f32)
        back = lambda x: pltpu.roll(x, 128 - BLOCK, 1)
        ahead = lambda x: pltpu.roll(x, BLOCK, 1)
        at = slice(i * wide, (i + 2) * wide)
        f_mid[:, at] = jnp.where(lane < wide, back(even), ahead(odd)).astype(bf16)
        f_edge[:, at] = jnp.where(lane < wide, ahead(even), back(odd)).astype(bf16)


def middle_kernel(nlat_all, taps, f_ref, main, near, far, rest, band, f_edge, q_ref, total, window, lines, f_mid, ext):
    lat_dev, lon_dev, channels = main.shape
    half, side = near.shape[0], BLOCK // 2
    inner = window.shape[2]
    above, start, _ = held_rows(lat_dev, half, nlat_all)
    build_band(above - start, taps, band, lines)
    cut_fields(f_ref, f_mid, f_edge)
    ext[half : half + lat_dev] = main[...]
    odd_lat = parity(LAT)
    for upper in (0, 1):

        @pl.when(odd_lat != upper)
        def _():
            above, below = slice(0, half), slice(half + lat_dev, None)
            ext[below if upper else above] = near[...]
            other = above if upper else below
            ext[other, :side, :] = far[:, :side, :]
            ext[other, side : lon_dev - side, :] = rest[...]
            ext[other, lon_dev - side :, :] = far[:, side:, :]

    window[:, 0] = ext[:, lon_dev - inner :, :]
    window[:, 1] = ext[:, :inner, :]
    convolve(band, ext, lambda j: (slice(side + j * BLOCK, side + (j + 2) * BLOCK),), q_ref)
    for k in range(q_ref.shape[0]):
        cells = q_ref[k].reshape(f_mid.shape[1], channels)
        total[k] = jnp.dot(f_mid[...], cells, preferred_element_type=f32)


def edge_kernel(band, window, far, near, corner, f_ref, total, w_ref, q_ref, low, high, w_out, ext, sem):
    fetch = pltpu.make_async_copy(w_ref, w_out, sem)
    fetch.start()
    channels = window.shape[3]
    side, inner = near.shape[1], window.shape[2]
    ext[:, 0, :inner, :] = window[:, 0]
    ext[:, 1, side:, :] = window[:, 1]
    odd_lon, odd_lat = parity(LON), parity(LAT)
    half, held = corner.shape[0], far.shape[0]
    for odd, (rows, rest) in enumerate(((slice(0, held), slice(held, None)), (slice(half, None), slice(0, half)))):
        for even in (0, 1):

            @pl.when((odd_lon != even) & (odd_lat == odd))
            def _():
                right, left = (near, far) if even else (far, near)
                ext[rows, 0, inner:, :] = right[...]
                ext[rows, 1, :side, :] = left[...]
                ext[rest, 0, inner:, :] = corner[:, side:] if even else corner[:, :side]
                ext[rest, 1, :side, :] = corner[:, :side] if even else corner[:, side:]

    convolve(band, ext, lambda j: (j,), q_ref)
    for k in range(q_ref.shape[0]):
        cells = q_ref[k].reshape(f_ref.shape[1], channels)
        out = total[k] + jnp.dot(f_ref[...], cells, preferred_element_type=f32)
        low[k] = out[:, : channels // 2]
        high[k] = out[:, channels // 2 :]
    fetch.wait()


def call(kernel, out_shape, operands, scratch=(), hbm=0, flops=10**9, mib=16):
    vmem = pl.BlockSpec(memory_space=pltpu.VMEM)
    return pl.pallas_call(
        kernel,
        out_shape=out_shape,
        in_specs=[vmem] * (len(operands) - hbm) + [pl.BlockSpec(memory_space=pl.ANY)] * hbm,
        out_specs=jax.tree.map(lambda _: vmem, out_shape),
        scratch_shapes=list(scratch),
        compiler_params=pltpu.CompilerParams(vmem_limit_bytes=mib * 1024 * 1024),
        cost_estimate=pl.CostEstimate(flops=flops, bytes_accessed=10**6, transcendentals=0),
    )(*operands)


def mix_kernel(w_ref, mid_ref, edge_ref, out_ref):
    basis_count, lat_dev, columns, channels = mid_ref.shape
    for i in range(0, lat_dev, 2):
        total = jnp.zeros((channels, 4 * columns), f32)
        for k in range(basis_count):
            parts = []
            for row in (i, i + 1):
                parts += [edge_ref[k, row, BLOCK:], mid_ref[k, row], edge_ref[k, row, :BLOCK]]
            total += lax.dot_general(
                w_ref[k], jnp.concatenate(parts, axis=0), (((1,), (1,)), ((), ())), preferred_element_type=f32
            )
        out_ref[:, i * 2 * columns : (i + 2) * 2 * columns] = total.astype(bf16)


def place_kernel(own, half_ref, *refs):
    out, wide, sems = refs[-3:]
    basis_count, _, columns = half_ref.shape
    at = lax.axis_index("core") if own else 1 - lax.axis_index("core")
    at = pl.ds(pl.multiple_of(at * columns, columns), columns)
    parts = sems.shape[0]
    size = basis_count // parts
    copies = []
    for part in range(parts):
        rows = slice(part * size, (part + 1) * size)
        wide[rows] = half_ref[rows].astype(f32)
        copies.append(pltpu.make_async_copy(wide.at[rows], out.at[rows, :, at], sems.at[part]))
        copies[-1].start()
    for copy in copies:
        copy.wait()


def place(half, own, into=None):
    basis_count, channels, columns = half.shape
    hbm = pl.BlockSpec(memory_space=pl.ANY)
    operands = (half,) if into is None else (half, into)
    return pl.pallas_call(
        functools.partial(place_kernel, own),
        out_shape=jax.ShapeDtypeStruct((basis_count, channels, 2 * columns), f32),
        in_specs=[pl.BlockSpec(memory_space=pltpu.VMEM)] + [hbm] * (len(operands) - 1),
        out_specs=hbm,
        scratch_shapes=[pltpu.VMEM(half.shape, f32), pltpu.SemaphoreType.DMA((3,))],
        input_output_aliases={} if into is None else {1: 0},
        compiler_params=pltpu.CompilerParams(vmem_limit_bytes=4 * 1024 * 1024),
        cost_estimate=pl.CostEstimate(flops=10**6, bytes_accessed=10**6, transcendentals=0),
    )(*operands)


def all_to_all(x, axes):
    return lax.all_to_all(x, axes, 0, 0, tiled=True)


def to_all(x, count):
    return jnp.broadcast_to(x[None], (count,) + x.shape)


def reduce_all(low, high, core, scale, beside, finish):
    swap = [(0, 1), (1, 0)]
    basis_count, channels, half = low.shape
    plane = 1
    for axis in PLANE:
        plane *= lax.axis_size(axis)
    depth = lax.axis_size("z")
    keep, send = jnp.where(core == 0, low, high), jnp.where(core == 0, high, low).astype(bf16)
    came, beside = lax.optimization_barrier((lax.ppermute(send, "core", swap), beside))
    own = keep + came.astype(f32)
    own = own.reshape(plane, -1, half).astype(bf16)
    own = jnp.sum(all_to_all(own, PLANE).astype(f32), axis=0).astype(bf16)
    own = jnp.sum(all_to_all(to_all(own, depth), ("z",)).astype(f32), axis=0)
    own = (own * scale).astype(bf16)
    own = all_to_all(to_all(own, plane), PLANE).reshape(basis_count, channels, half)
    beside = finish(beside)
    other, summed, beside = lax.optimization_barrier((lax.ppermute(own, "core", swap), place(own, True), beside))
    return place(other, False, summed), beside


def local(fields, grad_out, weight, basis_table, lon_reach):
    channels, lat_dev, lon_dev = fields.shape
    basis_count, nlat_all, row_span, tap_count = basis_table.shape
    half, side = row_span // 2, tap_count // 2
    near, wide = lat_dev + 2 * half, 2 * BLOCK
    shape = jax.ShapeDtypeStruct
    core = lax.axis_index("core")
    _, start, held = held_rows(lat_dev, half, nlat_all)
    upper = core == 0
    main = jnp.transpose(grad_out, (1, 2, 0))
    last, first = main[lat_dev - half :], main[:half]
    to_near, to_far = jnp.where(upper, last, first), jnp.where(upper, first, last)
    outer = jnp.concatenate([to_far[:, :side], to_far[:, lon_dev - side :]], axis=1)
    far_lat = lax.ppermute(outer, LAT, pairs(LAT, False, False))
    rest_lat = lax.ppermute(to_far[:, side : lon_dev - side], LAT, pairs(LAT, False, False))
    rim = shape((near - half, side, channels), bf16)
    second, first = call(rim_kernel, (rim, rim), (main, far_lat), flops=10**6, mib=4)
    to_near, second, first = lax.optimization_barrier((to_near, second, first))
    far_lon = lax.ppermute(second, LON, pairs(LON, False, True))
    near_lon = lax.ppermute(first, LON, pairs(LON, True, True))
    near_lat = lax.ppermute(to_near, LAT, pairs(LAT, True, False))
    taps = tap_rows(basis_table, lon_reach, start, held)
    q_shape = shape((basis_count, lat_dev, wide, channels), bf16)
    columns = shape((channels, lat_dev * wide), bf16)
    part = shape((basis_count, channels, channels // 2), f32)
    band, f_edge, q_mid, total, window = call(
        functools.partial(middle_kernel, nlat_all),
        (
            shape((lat_dev, basis_count * BLOCK, (row_span + 1) * wide), bf16),
            columns,
            q_shape,
            shape((basis_count, channels, channels), f32),
            shape((near, 2, wide - side, channels), bf16),
        ),
        (taps, fields.reshape(channels, lat_dev * lon_dev), main, near_lat, far_lat, rest_lat),
        [
            pltpu.VMEM((basis_count, row_span, held + 16, 128), f32),
            pltpu.VMEM(columns.shape, bf16),
            pltpu.VMEM((near, lon_dev, channels), bf16),
        ],
    )
    far_lon, near_lon, total = lax.optimization_barrier((far_lon, near_lon, total))
    corner = call(corner_kernel, shape((half, 2 * side, channels), bf16), (far_lon, near_lon), flops=10**6, mib=4)
    corner = lax.ppermute(corner, LAT, pairs(LAT, True, False))
    q_edge, low, high, weight = call(
        edge_kernel,
        (q_shape, part, part, shape(weight.shape, bf16)),
        (band, window, far_lon, near_lon, corner, f_edge, total, weight),
        [pltpu.VMEM((near, 2, wide, channels), bf16), pltpu.SemaphoreType.DMA],
        hbm=1,
    )
    mixed = call(mix_kernel, shape((channels, lat_dev * lon_dev), bf16), (weight, q_mid, q_edge))
    weight_grad, field_grad = reduce_all(
        low, high, core, 1.0 / nlat_all, mixed, lambda x: x.reshape(channels, lat_dev, lon_dev)
    )
    return field_grad, weight_grad


def solution(mesh):
    fine = Mesh(mesh.devices.reshape(4, 2, 2, 8, 2), ("y", "x_lo", "core", "z", "x_hi"))
    split = P(None, LAT, LON)
    return jax.shard_map(
        local,
        mesh=fine,
        in_specs=(split, split, P(), P(), P()),
        out_specs=(split, P()),
        check_vma=False,
    )
```

```python
import functools

import jax
import jax.numpy as jnp
from jax import lax
from jax.experimental import pallas as pl
from jax.experimental.pallas import tpu as pltpu
from jax.sharding import Mesh, PartitionSpec as P

LAT = ("y", "x_lo", "core")
LON = ("z", "x_hi")
PLANE = ("y", "x_hi", "x_lo")
BLOCK = 32
bf16, f32 = jnp.bfloat16, jnp.float32


def pairs(axes, near, closed):
    count = 1
    for axis in axes:
        count *= lax.axis_size(axis)
    if near:
        return [(i, i ^ 1) for i in range(count)]
    far = [(i, (i + 1 - 2 * (i % 2 == 0)) % count) for i in range(count)]
    return far if closed else far[1:-1]


def parity(axes):
    return lax.rem(lax.axis_index(axes[-1]), 2)


def held_rows(lat_dev, half, nlat_all):
    above = lax.axis_index(LAT) * lat_dev - half
    held = min(16, nlat_all)
    return above, jnp.clip(above, 0, nlat_all - held), held


def mask_taps(table, reach):
    tap_count = table.shape[3]
    offset = jnp.abs(lax.iota(jnp.int32, tap_count) - tap_count // 2)
    table = jnp.where((offset[None, :] <= reach[:, None])[None, :, None, :], table, jnp.zeros_like(table))
    return jnp.transpose(table, (0, 2, 1, 3))


def own_rows(half, lat_dev):
    return (slice(half, half + lat_dev), slice(0, half)), (slice(0, lat_dev), slice(lat_dev, None))


def rim_kernel(main, far, second, first):
    lat_dev, lon_dev, _ = main.shape
    half, side = far.shape[0], first.shape[1]
    odd_lon, odd_lat = parity(LON), parity(LAT)
    last = lon_dev - side
    for odd, (own, other) in enumerate(own_rows(half, lat_dev)):
        for even in (0, 1):

            @pl.when((odd_lon != even) & (odd_lat == odd))
            def _():
                for ref, at in ((first, last if even else 0), (second, 0 if even else last)):
                    outer = slice(side, 2 * side) if at else slice(0, side)
                    ref[own] = main[:, at : at + side, :]
                    ref[other] = far[:, outer, :]


def corner_kernel(far, near, out):
    half, side = out.shape[0], far.shape[1]
    lat_dev = far.shape[0] - half
    odd_lat = parity(LAT)
    for odd, rows in enumerate((slice(lat_dev, None), slice(0, half))):

        @pl.when(odd_lat == odd)
        def _():
            out[:, :side, :] = far[rows]
            out[:, side:, :] = near[rows]


def convolve(band, ext, place, q_ref):
    basis_count, lat_dev, columns, _ = q_ref.shape
    row_span = ext.shape[0] - lat_dev + 1
    for i in range(lat_dev):
        for j in range(columns // BLOCK):
            parts = [ext[(i + row_span - 1 - s,) + place(j)] for s in range(row_span)]
            window = jnp.concatenate(parts + [jnp.zeros_like(parts[0])], axis=0)
            out = jnp.dot(band[i], window, preferred_element_type=f32).astype(bf16)
            for k in range(basis_count):
                q_ref[k, i, j * BLOCK : (j + 1) * BLOCK, :] = out[k * BLOCK : (k + 1) * BLOCK, :]


def build_band(off, taps, band, lines):
    basis_count, row_span, near, tap_count = taps.shape
    lat_dev = band.shape[0]
    wide = 2 * BLOCK
    tap = lax.broadcasted_iota(jnp.int32, (tap_count, 128), 0)
    lane = lax.broadcasted_iota(jnp.int32, (tap_count, 128), 1)
    lines[...] = jnp.zeros_like(lines)
    for s in range(row_span):
        turn = (lane == s % 2 * wide + tap_count - 1 - tap).astype(bf16)
        for k in range(basis_count):
            lines[k, s, 8 : 8 + near, :] = jnp.dot(taps[k, s], turn, preferred_element_type=f32)
    base = off + 8 + row_span - 1
    for k in range(basis_count):
        for p in range((row_span + 1) // 2):
            pair = lines[k, 2 * p, pl.ds(base - 2 * p, lat_dev), :]
            if 2 * p + 1 < row_span:
                pair = pair + lines[k, 2 * p + 1, pl.ds(base - 2 * p - 1, lat_dev), :]
            for i in range(lat_dev):
                line = jnp.broadcast_to(pair[i : i + 1, :], (BLOCK, 128))
                line = pltpu.roll(line, 0, 1, stride=1, stride_axis=0)
                band[i, k * BLOCK : (k + 1) * BLOCK, p * 128 : (p + 1) * 128] = line.astype(bf16)


def cut_fields(f_ref, f_mid, f_edge):
    wide = 2 * BLOCK
    lane = lax.broadcasted_iota(jnp.int32, (1, 128), 1)
    for i in range(0, f_ref.shape[1] // 128, 2):
        even = f_ref[:, i * 128 : (i + 1) * 128].astype(f32)
        odd = f_ref[:, (i + 1) * 128 : (i + 2) * 128].astype(f32)
        back = lambda x: pltpu.roll(x, 128 - BLOCK, 1)
        ahead = lambda x: pltpu.roll(x, BLOCK, 1)
        at = slice(i * wide, (i + 2) * wide)
        f_mid[:, at] = jnp.where(lane < wide, back(even), ahead(odd)).astype(bf16)
        f_edge[:, at] = jnp.where(lane < wide, ahead(even), back(odd)).astype(bf16)


def middle_kernel(nlat_all, taps, f_ref, main, near, far, rest, band, f_edge, q_ref, total, window, lines, f_mid, ext):
    lat_dev, lon_dev, channels = main.shape
    half, side = near.shape[0], BLOCK // 2
    inner = window.shape[2]
    above, start, _ = held_rows(lat_dev, half, nlat_all)
    build_band(above - start, taps, band, lines)
    cut_fields(f_ref, f_mid, f_edge)
    ext[half : half + lat_dev] = main[...]
    odd_lat = parity(LAT)
    for upper in (0, 1):

        @pl.when(odd_lat != upper)
        def _():
            above, below = slice(0, half), slice(half + lat_dev, None)
            ext[below if upper else above] = near[...]
            other = above if upper else below
            ext[other, :side, :] = far[:, :side, :]
            ext[other, side : lon_dev - side, :] = rest[...]
            ext[other, lon_dev - side :, :] = far[:, side:, :]

    window[:, 0] = ext[:, lon_dev - inner :, :]
    window[:, 1] = ext[:, :inner, :]
    convolve(band, ext, lambda j: (slice(side + j * BLOCK, side + (j + 2) * BLOCK),), q_ref)
    for k in range(q_ref.shape[0]):
        cells = q_ref[k].reshape(f_mid.shape[1], channels)
        total[k] = jnp.dot(f_mid[...], cells, preferred_element_type=f32)


def edge_kernel(band, window, far, near, corner, f_ref, total, w_ref, q_ref, low, high, w_out, ext, sem):
    fetch = pltpu.make_async_copy(w_ref, w_out, sem)
    fetch.start()
    channels = window.shape[3]
    side, inner = near.shape[1], window.shape[2]
    ext[:, 0, :inner, :] = window[:, 0]
    ext[:, 1, side:, :] = window[:, 1]
    odd_lon, odd_lat = parity(LON), parity(LAT)
    half, held = corner.shape[0], far.shape[0]
    for odd, (rows, rest) in enumerate(((slice(0, held), slice(held, None)), (slice(half, None), slice(0, half)))):
        for even in (0, 1):

            @pl.when((odd_lon != even) & (odd_lat == odd))
            def _():
                right, left = (near, far) if even else (far, near)
                ext[rows, 0, inner:, :] = right[...]
                ext[rows, 1, :side, :] = left[...]
                ext[rest, 0, inner:, :] = corner[:, side:] if even else corner[:, :side]
                ext[rest, 1, :side, :] = corner[:, :side] if even else corner[:, side:]

    convolve(band, ext, lambda j: (j,), q_ref)
    for k in range(q_ref.shape[0]):
        cells = q_ref[k].reshape(f_ref.shape[1], channels)
        out = total[k] + jnp.dot(f_ref[...], cells, preferred_element_type=f32)
        low[k] = out[:, : channels // 2]
        high[k] = out[:, channels // 2 :]
    fetch.wait()


def call(kernel, out_shape, operands, scratch=(), hbm=0, flops=10**9, mib=16):
    vmem = pl.BlockSpec(memory_space=pltpu.VMEM)
    return pl.pallas_call(
        kernel,
        out_shape=out_shape,
        in_specs=[vmem] * (len(operands) - hbm) + [pl.BlockSpec(memory_space=pl.ANY)] * hbm,
        out_specs=jax.tree.map(lambda _: vmem, out_shape),
        scratch_shapes=list(scratch),
        compiler_params=pltpu.CompilerParams(vmem_limit_bytes=mib * 1024 * 1024),
        cost_estimate=pl.CostEstimate(flops=flops, bytes_accessed=10**6, transcendentals=0),
    )(*operands)


def mix_kernel(w_ref, mid_ref, edge_ref, out_ref):
    basis_count, lat_dev, columns, channels = mid_ref.shape
    for i in range(0, lat_dev, 2):
        total = jnp.zeros((channels, 4 * columns), f32)
        for k in range(basis_count):
            parts = []
            for row in (i, i + 1):
                parts += [edge_ref[k, row, BLOCK:], mid_ref[k, row], edge_ref[k, row, :BLOCK]]
            total += lax.dot_general(
                w_ref[k], jnp.concatenate(parts, axis=0), (((1,), (1,)), ((), ())), preferred_element_type=f32
            )
        out_ref[:, i * 2 * columns : (i + 2) * 2 * columns] = total.astype(bf16)


def place_kernel(own, half_ref, *refs):
    out, wide, sems = refs[-3:]
    basis_count, _, columns = half_ref.shape
    at = lax.axis_index("core") if own else 1 - lax.axis_index("core")
    at = pl.ds(pl.multiple_of(at * columns, columns), columns)
    parts = sems.shape[0]
    size = basis_count // parts
    copies = []
    for part in range(parts):
        rows = slice(part * size, (part + 1) * size)
        wide[rows] = half_ref[rows].astype(f32)
        copies.append(pltpu.make_async_copy(wide.at[rows], out.at[rows, :, at], sems.at[part]))
        copies[-1].start()
    for copy in copies:
        copy.wait()


def place(half, own, into=None):
    basis_count, channels, columns = half.shape
    hbm = pl.BlockSpec(memory_space=pl.ANY)
    operands = (half,) if into is None else (half, into)
    return pl.pallas_call(
        functools.partial(place_kernel, own),
        out_shape=jax.ShapeDtypeStruct((basis_count, channels, 2 * columns), f32),
        in_specs=[pl.BlockSpec(memory_space=pltpu.VMEM)] + [hbm] * (len(operands) - 1),
        out_specs=hbm,
        scratch_shapes=[pltpu.VMEM(half.shape, f32), pltpu.SemaphoreType.DMA((3,))],
        input_output_aliases={} if into is None else {1: 0},
        compiler_params=pltpu.CompilerParams(vmem_limit_bytes=4 * 1024 * 1024),
        cost_estimate=pl.CostEstimate(flops=10**6, bytes_accessed=10**6, transcendentals=0),
    )(*operands)


def all_to_all(x, axes):
    return lax.all_to_all(x, axes, 0, 0, tiled=True)


def to_all(x, count):
    return jnp.broadcast_to(x[None], (count,) + x.shape)


def reduce_all(low, high, core, scale, beside, finish):
    swap = [(0, 1), (1, 0)]
    basis_count, channels, half = low.shape
    plane = 1
    for axis in PLANE:
        plane *= lax.axis_size(axis)
    depth = lax.axis_size("z")
    keep, send = jnp.where(core == 0, low, high), jnp.where(core == 0, high, low).astype(bf16)
    came, beside = lax.optimization_barrier((lax.ppermute(send, "core", swap), beside))
    own = keep + came.astype(f32)
    own = own.reshape(plane, -1, half).astype(bf16)
    own = jnp.sum(all_to_all(own, PLANE).astype(f32), axis=0).astype(bf16)
    own = jnp.sum(all_to_all(to_all(own, depth), ("z",)).astype(f32), axis=0)
    own = (own * scale).astype(bf16)
    own = all_to_all(to_all(own, plane), PLANE).reshape(basis_count, channels, half)
    beside = finish(beside)
    other, summed, beside = lax.optimization_barrier((lax.ppermute(own, "core", swap), place(own, True), beside))
    return place(other, False, summed), beside


def local(fields, grad_out, weight, basis_table, lon_reach):
    channels, lat_dev, lon_dev = fields.shape
    basis_count, nlat_all, row_span, tap_count = basis_table.shape
    half, side = row_span // 2, tap_count // 2
    near, wide = lat_dev + 2 * half, 2 * BLOCK
    shape = jax.ShapeDtypeStruct
    core = lax.axis_index("core")
    _, start, held = held_rows(lat_dev, half, nlat_all)
    upper = core == 0
    main = jnp.transpose(grad_out, (1, 2, 0))
    last, first = main[lat_dev - half :], main[:half]
    to_near, to_far = jnp.where(upper, last, first), jnp.where(upper, first, last)
    outer = jnp.concatenate([to_far[:, :side], to_far[:, lon_dev - side :]], axis=1)
    far_lat = lax.ppermute(outer, LAT, pairs(LAT, False, False))
    rest_lat = lax.ppermute(to_far[:, side : lon_dev - side], LAT, pairs(LAT, False, False))
    rim = shape((near - half, side, channels), bf16)
    second, first = call(rim_kernel, (rim, rim), (main, far_lat), flops=10**6, mib=4)
    start, to_near, second, first = lax.optimization_barrier((start, to_near, second, first))
    table = lax.dynamic_slice_in_dim(basis_table, start, held, 1)
    reach = lax.dynamic_slice_in_dim(lon_reach, start, held, 0)
    taps = mask_taps(table, reach)
    far_lon = lax.ppermute(second, LON, pairs(LON, False, True))
    near_lon = lax.ppermute(first, LON, pairs(LON, True, True))
    near_lat = lax.ppermute(to_near, LAT, pairs(LAT, True, False))
    q_shape = shape((basis_count, lat_dev, wide, channels), bf16)
    columns = shape((channels, lat_dev * wide), bf16)
    part = shape((basis_count, channels, channels // 2), f32)
    band, f_edge, q_mid, total, window = call(
        functools.partial(middle_kernel, nlat_all),
        (
            shape((lat_dev, basis_count * BLOCK, (row_span + 1) * wide), bf16),
            columns,
            q_shape,
            shape((basis_count, channels, channels), f32),
            shape((near, 2, wide - side, channels), bf16),
        ),
        (taps, fields.reshape(channels, lat_dev * lon_dev), main, near_lat, far_lat, rest_lat),
        [
            pltpu.VMEM((basis_count, row_span, held + 16, 128), f32),
            pltpu.VMEM(columns.shape, bf16),
            pltpu.VMEM((near, lon_dev, channels), bf16),
        ],
    )
    far_lon, near_lon, total = lax.optimization_barrier((far_lon, near_lon, total))
    corner = call(corner_kernel, shape((half, 2 * side, channels), bf16), (far_lon, near_lon), flops=10**6, mib=4)
    corner = lax.ppermute(corner, LAT, pairs(LAT, True, False))
    q_edge, low, high, weight = call(
        edge_kernel,
        (q_shape, part, part, shape(weight.shape, bf16)),
        (band, window, far_lon, near_lon, corner, f_edge, total, weight),
        [pltpu.VMEM((near, 2, wide, channels), bf16), pltpu.SemaphoreType.DMA],
        hbm=1,
    )
    mixed = call(mix_kernel, shape((channels, lat_dev * lon_dev), bf16), (weight, q_mid, q_edge))
    weight_grad, field_grad = reduce_all(
        low, high, core, 1.0 / nlat_all, mixed, lambda x: x.reshape(channels, lat_dev, lon_dev)
    )
    return field_grad, weight_grad


def solution(mesh):
    fine = Mesh(mesh.devices.reshape(4, 2, 2, 8, 2), ("y", "x_lo", "core", "z", "x_hi"))
    split = P(None, LAT, LON)
    return jax.shard_map(
        local,
        mesh=fine,
        in_specs=(split, split, P(), P(), P()),
        out_specs=(split, P()),
        check_vma=False,
    )
```

```python
import functools

import jax
import jax.numpy as jnp
from jax import lax
from jax.experimental import pallas as pl
from jax.experimental.pallas import tpu as pltpu
from jax.sharding import Mesh, PartitionSpec as P

LAT = ("y", "x_lo", "core")
LON = ("z", "x_hi")
PLANE = ("y", "x_hi", "x_lo")
BLOCK = 32
bf16, f32 = jnp.bfloat16, jnp.float32


def pairs(axes, near, closed):
    count = 1
    for axis in axes:
        count *= lax.axis_size(axis)
    if near:
        return [(i, i ^ 1) for i in range(count)]
    far = [(i, (i + 1 - 2 * (i % 2 == 0)) % count) for i in range(count)]
    return far if closed else far[1:-1]


def parity(axes):
    return lax.rem(lax.axis_index(axes[-1]), 2)


def held_rows(lat_dev, half, nlat_all):
    above = lax.axis_index(LAT) * lat_dev - half
    held = min(16, nlat_all)
    return above, jnp.clip(above, 0, nlat_all - held), held


def mask_taps(table, reach):
    tap_count = table.shape[3]
    offset = jnp.abs(lax.iota(jnp.int32, tap_count) - tap_count // 2)
    table = jnp.where((offset[None, :] <= reach[:, None])[None, :, None, :], table, jnp.zeros_like(table))
    return jnp.transpose(table, (0, 2, 1, 3))


def own_rows(half, lat_dev):
    return (slice(half, half + lat_dev), slice(0, half)), (slice(0, lat_dev), slice(lat_dev, None))


def rim_kernel(main, far, second, first):
    lat_dev, lon_dev, _ = main.shape
    half, side = far.shape[0], first.shape[1]
    odd_lon, odd_lat = parity(LON), parity(LAT)
    last = lon_dev - side
    for odd, (own, other) in enumerate(own_rows(half, lat_dev)):
        for even in (0, 1):

            @pl.when((odd_lon != even) & (odd_lat == odd))
            def _():
                for ref, at in ((first, last if even else 0), (second, 0 if even else last)):
                    outer = slice(side, 2 * side) if at else slice(0, side)
                    ref[own] = main[:, at : at + side, :]
                    ref[other] = far[:, outer, :]


def cut_kernel(main, outer, rest, to_near):
    lat_dev, lon_dev, _ = main.shape
    half, side = outer.shape[0], outer.shape[1] // 2
    odd_lat = parity(LAT)
    first, last = slice(0, half), slice(lat_dev - half, lat_dev)
    for odd, (far, near) in enumerate(((first, last), (last, first))):

        @pl.when(odd_lat == odd)
        def _():
            outer[:, :side] = main[far, :side]
            outer[:, side:] = main[far, lon_dev - side :]
            rest[...] = main[far, side : lon_dev - side]
            to_near[...] = main[near]


def corner_kernel(far, near, out):
    half, side = out.shape[0], far.shape[1]
    lat_dev = far.shape[0] - half
    odd_lat = parity(LAT)
    for odd, rows in enumerate((slice(lat_dev, None), slice(0, half))):

        @pl.when(odd_lat == odd)
        def _():
            out[:, :side, :] = far[rows]
            out[:, side:, :] = near[rows]


def convolve(band, ext, place, q_ref):
    basis_count, lat_dev, columns, _ = q_ref.shape
    row_span = ext.shape[0] - lat_dev + 1
    for i in range(lat_dev):
        for j in range(columns // BLOCK):
            parts = [ext[(i + row_span - 1 - s,) + place(j)] for s in range(row_span)]
            window = jnp.concatenate(parts + [jnp.zeros_like(parts[0])], axis=0)
            out = jnp.dot(band[i], window, preferred_element_type=f32).astype(bf16)
            for k in range(basis_count):
                q_ref[k, i, j * BLOCK : (j + 1) * BLOCK, :] = out[k * BLOCK : (k + 1) * BLOCK, :]


def build_band(off, taps, band, lines):
    basis_count, row_span, near, tap_count = taps.shape
    lat_dev = band.shape[0]
    wide = 2 * BLOCK
    tap = lax.broadcasted_iota(jnp.int32, (tap_count, 128), 0)
    lane = lax.broadcasted_iota(jnp.int32, (tap_count, 128), 1)
    lines[...] = jnp.zeros_like(lines)
    for s in range(row_span):
        turn = (lane == s % 2 * wide + tap_count - 1 - tap).astype(bf16)
        for k in range(basis_count):
            lines[k, s, 8 : 8 + near, :] = jnp.dot(taps[k, s], turn, preferred_element_type=f32)
    base = off + 8 + row_span - 1
    for k in range(basis_count):
        for p in range((row_span + 1) // 2):
            pair = lines[k, 2 * p, pl.ds(base - 2 * p, lat_dev), :]
            if 2 * p + 1 < row_span:
                pair = pair + lines[k, 2 * p + 1, pl.ds(base - 2 * p - 1, lat_dev), :]
            for i in range(lat_dev):
                line = jnp.broadcast_to(pair[i : i + 1, :], (BLOCK, 128))
                line = pltpu.roll(line, 0, 1, stride=1, stride_axis=0)
                band[i, k * BLOCK : (k + 1) * BLOCK, p * 128 : (p + 1) * 128] = line.astype(bf16)


def cut_fields(f_ref, f_mid, f_edge):
    wide = 2 * BLOCK
    lane = lax.broadcasted_iota(jnp.int32, (1, 128), 1)
    for i in range(0, f_ref.shape[1] // 128, 2):
        even = f_ref[:, i * 128 : (i + 1) * 128].astype(f32)
        odd = f_ref[:, (i + 1) * 128 : (i + 2) * 128].astype(f32)
        back = lambda x: pltpu.roll(x, 128 - BLOCK, 1)
        ahead = lambda x: pltpu.roll(x, BLOCK, 1)
        at = slice(i * wide, (i + 2) * wide)
        f_mid[:, at] = jnp.where(lane < wide, back(even), ahead(odd)).astype(bf16)
        f_edge[:, at] = jnp.where(lane < wide, ahead(even), back(odd)).astype(bf16)


def band_kernel(nlat_all, taps, band, lines):
    lat_dev = band.shape[0]
    above, start, _ = held_rows(lat_dev, taps.shape[1] // 2, nlat_all)
    build_band(above - start, taps, band, lines)


def middle_kernel(band, f_ref, main, near, far, rest, f_edge, q_ref, total, window, f_mid, ext):
    lat_dev, lon_dev, channels = main.shape
    half, side = near.shape[0], BLOCK // 2
    inner = window.shape[2]
    cut_fields(f_ref, f_mid, f_edge)
    ext[half : half + lat_dev] = main[...]
    odd_lat = parity(LAT)
    for upper in (0, 1):

        @pl.when(odd_lat != upper)
        def _():
            above, below = slice(0, half), slice(half + lat_dev, None)
            ext[below if upper else above] = near[...]
            other = above if upper else below
            ext[other, :side, :] = far[:, :side, :]
            ext[other, side : lon_dev - side, :] = rest[...]
            ext[other, lon_dev - side :, :] = far[:, side:, :]

    window[:, 0] = ext[:, lon_dev - inner :, :]
    window[:, 1] = ext[:, :inner, :]
    convolve(band, ext, lambda j: (slice(side + j * BLOCK, side + (j + 2) * BLOCK),), q_ref)
    for k in range(q_ref.shape[0]):
        cells = q_ref[k].reshape(f_mid.shape[1], channels)
        total[k] = jnp.dot(f_mid[...], cells, preferred_element_type=f32)


def edge_kernel(band, window, far, near, corner, f_ref, total, w_ref, q_ref, low, high, w_out, ext, sem):
    fetch = pltpu.make_async_copy(w_ref, w_out, sem)
    fetch.start()
    channels = window.shape[3]
    side, inner = near.shape[1], window.shape[2]
    ext[:, 0, :inner, :] = window[:, 0]
    ext[:, 1, side:, :] = window[:, 1]
    odd_lon, odd_lat = parity(LON), parity(LAT)
    half, held = corner.shape[0], far.shape[0]
    for odd, (rows, rest) in enumerate(((slice(0, held), slice(held, None)), (slice(half, None), slice(0, half)))):
        for even in (0, 1):

            @pl.when((odd_lon != even) & (odd_lat == odd))
            def _():
                right, left = (near, far) if even else (far, near)
                ext[rows, 0, inner:, :] = right[...]
                ext[rows, 1, :side, :] = left[...]
                ext[rest, 0, inner:, :] = corner[:, side:] if even else corner[:, :side]
                ext[rest, 1, :side, :] = corner[:, :side] if even else corner[:, side:]

    convolve(band, ext, lambda j: (j,), q_ref)
    for k in range(q_ref.shape[0]):
        cells = q_ref[k].reshape(f_ref.shape[1], channels)
        out = total[k] + jnp.dot(f_ref[...], cells, preferred_element_type=f32)
        low[k] = out[:, : channels // 2]
        high[k] = out[:, channels // 2 :]
    fetch.wait()


def call(kernel, out_shape, operands, scratch=(), hbm=0, flops=10**9, mib=16):
    vmem = pl.BlockSpec(memory_space=pltpu.VMEM)
    return pl.pallas_call(
        kernel,
        out_shape=out_shape,
        in_specs=[vmem] * (len(operands) - hbm) + [pl.BlockSpec(memory_space=pl.ANY)] * hbm,
        out_specs=jax.tree.map(lambda _: vmem, out_shape),
        scratch_shapes=list(scratch),
        compiler_params=pltpu.CompilerParams(vmem_limit_bytes=mib * 1024 * 1024),
        cost_estimate=pl.CostEstimate(flops=flops, bytes_accessed=10**6, transcendentals=0),
    )(*operands)


def mix_kernel(w_ref, mid_ref, edge_ref, out_ref):
    basis_count, lat_dev, columns, channels = mid_ref.shape
    for i in range(0, lat_dev, 2):
        total = jnp.zeros((channels, 4 * columns), f32)
        for k in range(basis_count):
            parts = []
            for row in (i, i + 1):
                parts += [edge_ref[k, row, BLOCK:], mid_ref[k, row], edge_ref[k, row, :BLOCK]]
            total += lax.dot_general(
                w_ref[k], jnp.concatenate(parts, axis=0), (((1,), (1,)), ((), ())), preferred_element_type=f32
            )
        out_ref[:, i * 2 * columns : (i + 2) * 2 * columns] = total.astype(bf16)


def place_kernel(own, half_ref, *refs):
    out, wide, sems = refs[-3:]
    basis_count, _, columns = half_ref.shape
    at = lax.axis_index("core") if own else 1 - lax.axis_index("core")
    at = pl.ds(pl.multiple_of(at * columns, columns), columns)
    parts = sems.shape[0]
    size = basis_count // parts
    copies = []
    for part in range(parts):
        rows = slice(part * size, (part + 1) * size)
        wide[rows] = half_ref[rows].astype(f32)
        copies.append(pltpu.make_async_copy(wide.at[rows], out.at[rows, :, at], sems.at[part]))
        copies[-1].start()
    for copy in copies:
        copy.wait()


def place(half, own, into=None):
    basis_count, channels, columns = half.shape
    hbm = pl.BlockSpec(memory_space=pl.ANY)
    operands = (half,) if into is None else (half, into)
    return pl.pallas_call(
        functools.partial(place_kernel, own),
        out_shape=jax.ShapeDtypeStruct((basis_count, channels, 2 * columns), f32),
        in_specs=[pl.BlockSpec(memory_space=pltpu.VMEM)] + [hbm] * (len(operands) - 1),
        out_specs=hbm,
        scratch_shapes=[pltpu.VMEM(half.shape, f32), pltpu.SemaphoreType.DMA((3,))],
        input_output_aliases={} if into is None else {1: 0},
        compiler_params=pltpu.CompilerParams(vmem_limit_bytes=4 * 1024 * 1024),
        cost_estimate=pl.CostEstimate(flops=10**6, bytes_accessed=10**6, transcendentals=0),
    )(*operands)


def all_to_all(x, axes):
    return lax.all_to_all(x, axes, 0, 0, tiled=True)


def to_all(x, count):
    return jnp.broadcast_to(x[None], (count,) + x.shape)


def reduce_all(low, high, core, scale, beside, finish):
    swap = [(0, 1), (1, 0)]
    basis_count, channels, half = low.shape
    plane = 1
    for axis in PLANE:
        plane *= lax.axis_size(axis)
    depth = lax.axis_size("z")
    keep, send = jnp.where(core == 0, low, high), jnp.where(core == 0, high, low).astype(bf16)
    came, beside = lax.optimization_barrier((lax.ppermute(send, "core", swap), beside))
    own = keep + came.astype(f32)
    own = own.reshape(plane, -1, half).astype(bf16)
    own = jnp.sum(all_to_all(own, PLANE).astype(f32), axis=0).astype(bf16)
    own = jnp.sum(all_to_all(to_all(own, depth), ("z",)).astype(f32), axis=0)
    own = (own * scale).astype(bf16)
    own = all_to_all(to_all(own, plane), PLANE).reshape(basis_count, channels, half)
    beside = finish(beside)
    other, summed, beside = lax.optimization_barrier((lax.ppermute(own, "core", swap), place(own, True), beside))
    return place(other, False, summed), beside


def local(fields, grad_out, weight, basis_table, lon_reach):
    channels, lat_dev, lon_dev = fields.shape
    basis_count, nlat_all, row_span, tap_count = basis_table.shape
    half, side = row_span // 2, tap_count // 2
    near, wide = lat_dev + 2 * half, 2 * BLOCK
    shape = jax.ShapeDtypeStruct
    core = lax.axis_index("core")
    _, start, held = held_rows(lat_dev, half, nlat_all)
    main = jnp.transpose(grad_out, (1, 2, 0))
    outer, rest, to_near = call(
        cut_kernel,
        tuple(shape((half, count, channels), bf16) for count in (2 * side, lon_dev - 2 * side, lon_dev)),
        (main,),
        flops=10**6,
        mib=4,
    )
    far_lat = lax.ppermute(outer, LAT, pairs(LAT, False, False))
    rest_lat = lax.ppermute(rest, LAT, pairs(LAT, False, False))
    rim = shape((near - half, side, channels), bf16)
    second, first = call(rim_kernel, (rim, rim), (main, far_lat), flops=10**6, mib=4)
    start, to_near, second, first = lax.optimization_barrier((start, to_near, second, first))
    table = lax.dynamic_slice_in_dim(basis_table, start, held, 1)
    reach = lax.dynamic_slice_in_dim(lon_reach, start, held, 0)
    taps = mask_taps(table, reach)
    far_lon = lax.ppermute(second, LON, pairs(LON, False, True))
    near_lon = lax.ppermute(first, LON, pairs(LON, True, True))
    near_lat = lax.ppermute(to_near, LAT, pairs(LAT, True, False))
    q_shape = shape((basis_count, lat_dev, wide, channels), bf16)
    columns = shape((channels, lat_dev * wide), bf16)
    part = shape((basis_count, channels, channels // 2), f32)
    band = call(
        functools.partial(band_kernel, nlat_all),
        shape((lat_dev, basis_count * BLOCK, (row_span + 1) * wide), bf16),
        (taps,),
        [pltpu.VMEM((basis_count, row_span, held + 16, 128), f32)],
        flops=10**8,
        mib=8,
    )
    f_edge, q_mid, total, window = call(
        middle_kernel,
        (
            columns,
            q_shape,
            shape((basis_count, channels, channels), f32),
            shape((near, 2, wide - side, channels), bf16),
        ),
        (band, fields.reshape(channels, lat_dev * lon_dev), main, near_lat, far_lat, rest_lat),
        [pltpu.VMEM(columns.shape, bf16), pltpu.VMEM((near, lon_dev, channels), bf16)],
    )
    far_lon, near_lon, total = lax.optimization_barrier((far_lon, near_lon, total))
    corner = call(corner_kernel, shape((half, 2 * side, channels), bf16), (far_lon, near_lon), flops=10**6, mib=4)
    corner = lax.ppermute(corner, LAT, pairs(LAT, True, False))
    q_edge, low, high, weight = call(
        edge_kernel,
        (q_shape, part, part, shape(weight.shape, bf16)),
        (band, window, far_lon, near_lon, corner, f_edge, total, weight),
        [pltpu.VMEM((near, 2, wide, channels), bf16), pltpu.SemaphoreType.DMA],
        hbm=1,
    )
    mixed = call(mix_kernel, shape((channels, lat_dev * lon_dev), bf16), (weight, q_mid, q_edge))
    weight_grad, field_grad = reduce_all(
        low, high, core, 1.0 / nlat_all, mixed, lambda x: x.reshape(channels, lat_dev, lon_dev)
    )
    return field_grad, weight_grad


def solution(mesh):
    fine = Mesh(mesh.devices.reshape(4, 2, 2, 8, 2), ("y", "x_lo", "core", "z", "x_hi"))
    split = P(None, LAT, LON)
    return jax.shard_map(
        local,
        mesh=fine,
        in_specs=(split, split, P(), P(), P()),
        out_specs=(split, P()),
        check_vma=False,
    )
```

```python
import functools

import jax
import jax.numpy as jnp
from jax import lax
from jax.experimental import pallas as pl
from jax.experimental.pallas import tpu as pltpu
from jax.sharding import Mesh, PartitionSpec as P

LAT = ("y", "x_lo", "core")
LON = ("z", "x_hi")
PLANE = ("y", "x_hi", "x_lo")
BLOCK = 32
bf16, f32 = jnp.bfloat16, jnp.float32


def pairs(axes, near, closed):
    count = 1
    for axis in axes:
        count *= lax.axis_size(axis)
    if near:
        return [(i, i ^ 1) for i in range(count)]
    far = [(i, (i + 1 - 2 * (i % 2 == 0)) % count) for i in range(count)]
    return far if closed else far[1:-1]


def parity(axes):
    return lax.rem(lax.axis_index(axes[-1]), 2)


def held_rows(lat_dev, half, nlat_all):
    above = lax.axis_index(LAT) * lat_dev - half
    held = min(16, nlat_all)
    return above, jnp.clip(above, 0, nlat_all - held), held


def mask_taps(table, reach):
    tap_count = table.shape[3]
    offset = jnp.abs(lax.iota(jnp.int32, tap_count) - tap_count // 2)
    table = jnp.where((offset[None, :] <= reach[:, None])[None, :, None, :], table, jnp.zeros_like(table))
    return jnp.transpose(table, (0, 2, 1, 3))


def own_rows(half, lat_dev):
    return (slice(half, half + lat_dev), slice(0, half)), (slice(0, lat_dev), slice(lat_dev, None))


def rim_kernel(main, far, second, first):
    lat_dev, lon_dev, _ = main.shape
    half, side = far.shape[0], first.shape[1]
    odd_lon, odd_lat = parity(LON), parity(LAT)
    last = lon_dev - side
    for odd, (own, other) in enumerate(own_rows(half, lat_dev)):
        for even in (0, 1):

            @pl.when((odd_lon != even) & (odd_lat == odd))
            def _():
                for ref, at in ((first, last if even else 0), (second, 0 if even else last)):
                    outer = slice(side, 2 * side) if at else slice(0, side)
                    ref[own] = main[:, at : at + side, :]
                    ref[other] = far[:, outer, :]


def corner_kernel(far, near, out):
    half, side = out.shape[0], far.shape[1]
    lat_dev = far.shape[0] - half
    odd_lat = parity(LAT)
    for odd, rows in enumerate((slice(lat_dev, None), slice(0, half))):

        @pl.when(odd_lat == odd)
        def _():
            out[:, :side, :] = far[rows]
            out[:, side:, :] = near[rows]


def convolve(band, ext, place, q_ref):
    basis_count, lat_dev, columns, _ = q_ref.shape
    row_span = ext.shape[0] - lat_dev + 1
    for i in range(lat_dev):
        for j in range(columns // BLOCK):
            parts = [ext[(i + row_span - 1 - s,) + place(j)] for s in range(row_span)]
            window = jnp.concatenate(parts + [jnp.zeros_like(parts[0])], axis=0)
            out = jnp.dot(band[i], window, preferred_element_type=f32).astype(bf16)
            for k in range(basis_count):
                q_ref[k, i, j * BLOCK : (j + 1) * BLOCK, :] = out[k * BLOCK : (k + 1) * BLOCK, :]


def build_band(off, taps, band, lines):
    basis_count, row_span, near, tap_count = taps.shape
    lat_dev = band.shape[0]
    wide = 2 * BLOCK
    tap = lax.broadcasted_iota(jnp.int32, (tap_count, 128), 0)
    lane = lax.broadcasted_iota(jnp.int32, (tap_count, 128), 1)
    lines[...] = jnp.zeros_like(lines)
    for s in range(row_span):
        turn = (lane == s % 2 * wide + tap_count - 1 - tap).astype(bf16)
        for k in range(basis_count):
            lines[k, s, 8 : 8 + near, :] = jnp.dot(taps[k, s], turn, preferred_element_type=f32)
    base = off + 8 + row_span - 1
    for k in range(basis_count):
        for p in range((row_span + 1) // 2):
            pair = lines[k, 2 * p, pl.ds(base - 2 * p, lat_dev), :]
            if 2 * p + 1 < row_span:
                pair = pair + lines[k, 2 * p + 1, pl.ds(base - 2 * p - 1, lat_dev), :]
            for i in range(lat_dev):
                line = jnp.broadcast_to(pair[i : i + 1, :], (BLOCK, 128))
                line = pltpu.roll(line, 0, 1, stride=1, stride_axis=0)
                band[i, k * BLOCK : (k + 1) * BLOCK, p * 128 : (p + 1) * 128] = line.astype(bf16)


def cut_fields(f_ref, f_mid, f_edge):
    wide = 2 * BLOCK
    lane = lax.broadcasted_iota(jnp.int32, (1, 128), 1)
    for i in range(0, f_ref.shape[1] // 128, 2):
        even = f_ref[:, i * 128 : (i + 1) * 128].astype(f32)
        odd = f_ref[:, (i + 1) * 128 : (i + 2) * 128].astype(f32)
        back = lambda x: pltpu.roll(x, 128 - BLOCK, 1)
        ahead = lambda x: pltpu.roll(x, BLOCK, 1)
        at = slice(i * wide, (i + 2) * wide)
        f_mid[:, at] = jnp.where(lane < wide, back(even), ahead(odd)).astype(bf16)
        f_edge[:, at] = jnp.where(lane < wide, ahead(even), back(odd)).astype(bf16)


def middle_kernel(nlat_all, taps, f_ref, main, near, far, rest, band, f_edge, q_ref, total, window, lines, f_mid, ext):
    lat_dev, lon_dev, channels = main.shape
    half, side = near.shape[0], BLOCK // 2
    inner = window.shape[2]
    above, start, _ = held_rows(lat_dev, half, nlat_all)
    build_band(above - start, taps, band, lines)
    cut_fields(f_ref, f_mid, f_edge)
    ext[half : half + lat_dev] = main[...]
    odd_lat = parity(LAT)
    for upper in (0, 1):

        @pl.when(odd_lat != upper)
        def _():
            above, below = slice(0, half), slice(half + lat_dev, None)
            ext[below if upper else above] = near[...]
            other = above if upper else below
            ext[other, :side, :] = far[:, :side, :]
            ext[other, side : lon_dev - side, :] = rest[...]
            ext[other, lon_dev - side :, :] = far[:, side:, :]

    window[:, 0] = ext[:, lon_dev - inner :, :]
    window[:, 1] = ext[:, :inner, :]
    convolve(band, ext, lambda j: (slice(side + j * BLOCK, side + (j + 2) * BLOCK),), q_ref)
    for k in range(q_ref.shape[0]):
        cells = q_ref[k].reshape(f_mid.shape[1], channels)
        total[k] = jnp.dot(f_mid[...], cells, preferred_element_type=f32)


def edge_kernel(band, window, far, near, corner, f_ref, total, w_ref, q_ref, low, high, w_out, ext, sem):
    fetch = pltpu.make_async_copy(w_ref, w_out, sem)
    fetch.start()
    channels = window.shape[3]
    side, inner = near.shape[1], window.shape[2]
    ext[:, 0, :inner, :] = window[:, 0]
    ext[:, 1, side:, :] = window[:, 1]
    odd_lon, odd_lat = parity(LON), parity(LAT)
    half, held = corner.shape[0], far.shape[0]
    for odd, (rows, rest) in enumerate(((slice(0, held), slice(held, None)), (slice(half, None), slice(0, half)))):
        for even in (0, 1):

            @pl.when((odd_lon != even) & (odd_lat == odd))
            def _():
                right, left = (near, far) if even else (far, near)
                ext[rows, 0, inner:, :] = right[...]
                ext[rows, 1, :side, :] = left[...]
                ext[rest, 0, inner:, :] = corner[:, side:] if even else corner[:, :side]
                ext[rest, 1, :side, :] = corner[:, :side] if even else corner[:, side:]

    convolve(band, ext, lambda j: (j,), q_ref)
    for k in range(q_ref.shape[0]):
        cells = q_ref[k].reshape(f_ref.shape[1], channels)
        out = total[k] + jnp.dot(f_ref[...], cells, preferred_element_type=f32)
        low[k] = out[:, : channels // 2]
        high[k] = out[:, channels // 2 :]
    fetch.wait()


def call(kernel, out_shape, operands, scratch=(), hbm=0, flops=10**9, mib=16):
    vmem = pl.BlockSpec(memory_space=pltpu.VMEM)
    return pl.pallas_call(
        kernel,
        out_shape=out_shape,
        in_specs=[vmem] * (len(operands) - hbm) + [pl.BlockSpec(memory_space=pl.ANY)] * hbm,
        out_specs=jax.tree.map(lambda _: vmem, out_shape),
        scratch_shapes=list(scratch),
        compiler_params=pltpu.CompilerParams(vmem_limit_bytes=mib * 1024 * 1024),
        cost_estimate=pl.CostEstimate(flops=flops, bytes_accessed=10**6, transcendentals=0),
    )(*operands)


def mix_kernel(w_ref, mid_ref, edge_ref, out_ref):
    basis_count, lat_dev, columns, channels = mid_ref.shape
    for i in range(0, lat_dev, 2):
        total = jnp.zeros((channels, 4 * columns), f32)
        for k in range(basis_count):
            parts = []
            for row in (i, i + 1):
                parts += [edge_ref[k, row, BLOCK:], mid_ref[k, row], edge_ref[k, row, :BLOCK]]
            total += lax.dot_general(
                w_ref[k], jnp.concatenate(parts, axis=0), (((1,), (1,)), ((), ())), preferred_element_type=f32
            )
        out_ref[:, i * 2 * columns : (i + 2) * 2 * columns] = total.astype(bf16)


def place_kernel(own, half_ref, *refs):
    out, wide, sems = refs[-3:]
    basis_count, _, columns = half_ref.shape
    at = lax.axis_index("core") if own else 1 - lax.axis_index("core")
    at = pl.ds(pl.multiple_of(at * columns, columns), columns)
    parts = sems.shape[0]
    size = basis_count // parts
    copies = []
    for part in range(parts):
        rows = slice(part * size, (part + 1) * size)
        wide[rows] = half_ref[rows].astype(f32)
        copies.append(pltpu.make_async_copy(wide.at[rows], out.at[rows, :, at], sems.at[part]))
        copies[-1].start()
    for copy in copies:
        copy.wait()


def place(half, own, into=None):
    basis_count, channels, columns = half.shape
    hbm = pl.BlockSpec(memory_space=pl.ANY)
    operands = (half,) if into is None else (half, into)
    return pl.pallas_call(
        functools.partial(place_kernel, own),
        out_shape=jax.ShapeDtypeStruct((basis_count, channels, 2 * columns), f32),
        in_specs=[pl.BlockSpec(memory_space=pltpu.VMEM)] + [hbm] * (len(operands) - 1),
        out_specs=hbm,
        scratch_shapes=[pltpu.VMEM(half.shape, f32), pltpu.SemaphoreType.DMA((3,))],
        input_output_aliases={} if into is None else {1: 0},
        compiler_params=pltpu.CompilerParams(vmem_limit_bytes=4 * 1024 * 1024),
        cost_estimate=pl.CostEstimate(flops=10**6, bytes_accessed=10**6, transcendentals=0),
    )(*operands)


def all_to_all(x, axes):
    return lax.all_to_all(x, axes, 0, 0, tiled=True)


def to_all(x, count):
    return jnp.broadcast_to(x[None], (count,) + x.shape)


def reduce_all(low, high, core, scale, beside, finish):
    swap = [(0, 1), (1, 0)]
    basis_count, channels, half = low.shape
    plane = 1
    for axis in PLANE:
        plane *= lax.axis_size(axis)
    depth = lax.axis_size("z")
    keep, send = jnp.where(core == 0, low, high), jnp.where(core == 0, high, low).astype(bf16)
    came, beside = lax.optimization_barrier((lax.ppermute(send, "core", swap), beside))
    own = keep + came.astype(f32)
    own = own.reshape(plane, -1, half).astype(bf16)
    own = jnp.sum(all_to_all(own, PLANE).astype(f32), axis=0).astype(bf16)
    own = jnp.sum(all_to_all(to_all(own, depth), ("z",)).astype(f32), axis=0)
    own = (own * scale).astype(bf16)
    own = all_to_all(to_all(own, plane), PLANE).reshape(basis_count, channels, half)
    beside = finish(beside)
    other, summed, beside = lax.optimization_barrier((lax.ppermute(own, "core", swap), place(own, True), beside))
    return place(other, False, summed), beside


def local(fields, grad_out, weight, basis_table, lon_reach):
    channels, lat_dev, lon_dev = fields.shape
    basis_count, nlat_all, row_span, tap_count = basis_table.shape
    half, side = row_span // 2, tap_count // 2
    near, wide = lat_dev + 2 * half, 2 * BLOCK
    shape = jax.ShapeDtypeStruct
    core = lax.axis_index("core")
    _, start, held = held_rows(lat_dev, half, nlat_all)
    upper = core == 0
    main = jnp.transpose(grad_out, (1, 2, 0))
    last, first = main[lat_dev - half :], main[:half]
    to_near, to_far = jnp.where(upper, last, first), jnp.where(upper, first, last)
    outer = jnp.concatenate([to_far[:, :side], to_far[:, lon_dev - side :]], axis=1)
    far_lat = lax.ppermute(outer, LAT, pairs(LAT, False, False))
    rest_lat = lax.ppermute(to_far[:, side : lon_dev - side], LAT, pairs(LAT, False, False))
    rim = shape((near - half, side, channels), bf16)
    second, first = call(rim_kernel, (rim, rim), (main, far_lat), flops=10**6, mib=4)
    table = lax.dynamic_slice_in_dim(basis_table, start, held, 1)
    reach = lax.dynamic_slice_in_dim(lon_reach, start, held, 0)
    table, to_near, second, first = lax.optimization_barrier((table, to_near, second, first))
    taps = mask_taps(table, reach)
    far_lon = lax.ppermute(second, LON, pairs(LON, False, True))
    near_lon = lax.ppermute(first, LON, pairs(LON, True, True))
    near_lat = lax.ppermute(to_near, LAT, pairs(LAT, True, False))
    q_shape = shape((basis_count, lat_dev, wide, channels), bf16)
    columns = shape((channels, lat_dev * wide), bf16)
    part = shape((basis_count, channels, channels // 2), f32)
    band, f_edge, q_mid, total, window = call(
        functools.partial(middle_kernel, nlat_all),
        (
            shape((lat_dev, basis_count * BLOCK, (row_span + 1) * wide), bf16),
            columns,
            q_shape,
            shape((basis_count, channels, channels), f32),
            shape((near, 2, wide - side, channels), bf16),
        ),
        (taps, fields.reshape(channels, lat_dev * lon_dev), main, near_lat, far_lat, rest_lat),
        [
            pltpu.VMEM((basis_count, row_span, held + 16, 128), f32),
            pltpu.VMEM(columns.shape, bf16),
            pltpu.VMEM((near, lon_dev, channels), bf16),
        ],
    )
    far_lon, near_lon, total = lax.optimization_barrier((far_lon, near_lon, total))
    corner = call(corner_kernel, shape((half, 2 * side, channels), bf16), (far_lon, near_lon), flops=10**6, mib=4)
    corner = lax.ppermute(corner, LAT, pairs(LAT, True, False))
    q_edge, low, high, weight = call(
        edge_kernel,
        (q_shape, part, part, shape(weight.shape, bf16)),
        (band, window, far_lon, near_lon, corner, f_edge, total, weight),
        [pltpu.VMEM((near, 2, wide, channels), bf16), pltpu.SemaphoreType.DMA],
        hbm=1,
    )
    mixed = call(mix_kernel, shape((channels, lat_dev * lon_dev), bf16), (weight, q_mid, q_edge))
    weight_grad, field_grad = reduce_all(
        low, high, core, 1.0 / nlat_all, mixed, lambda x: x.reshape(channels, lat_dev, lon_dev)
    )
    return field_grad, weight_grad


def solution(mesh):
    fine = Mesh(mesh.devices.reshape(4, 2, 2, 8, 2), ("y", "x_lo", "core", "z", "x_hi"))
    split = P(None, LAT, LON)
    return jax.shard_map(
        local,
        mesh=fine,
        in_specs=(split, split, P(), P(), P()),
        out_specs=(split, P()),
        check_vma=False,
    )
```
